128 devices in a mesh: expert: 16 (over z, y), tensor: 8 (over x, core).
Axes of the slice: x: 4, y: 4, z: 4, core: 2. Of those that a mesh axis runs over, the one named last changes fastest.
Arguments:
- layer_input: bfloat16 [4096, 2880], P('expert'), may hold values from -6 to 6
- segment_ids: int32 [4096], replicated, may hold values from 0 to 23, as said below
- expert_routes: int32 [4096, 4], P('expert'), may hold values from 0 to 31, all different within a row; in each aligned block of 256 rows (0 to 255, 256 to 511, ...) at most 48 rows name the same one
- attn_norm: float32 [2880], replicated, may hold values from 0.25 to 1.75
- q_weight: bfloat16 [4096, 2880], P('tensor', 'expert'), may hold values from -0.109375 to 0.109375
- q_bias: float32 [4096], P('tensor'), may hold values from -3 to 3
- key_matrix: bfloat16 [512, 2880], P('tensor', 'expert'), may hold values from -0.109375 to 0.109375
- key_bias: float32 [512], P('tensor'), may hold values from -3 to 3
- value_matrix: bfloat16 [512, 2880], P('tensor', 'expert'), may hold values from -0.109375 to 0.109375
- value_bias: float32 [512], P('tensor'), may hold values from -3 to 3
- o_weight: bfloat16 [4096, 2880], P('tensor', 'expert'), may hold values from -0.5 to 0.5
- o_bias: float32 [2880], replicated, may hold values from -3 to 3
- sink_scores: float32 [64], P('tensor'), may hold values from -3 to 3
- moe_norm: float32 [2880], replicated, may hold values from 0.25 to 1.75
- router_weight: bfloat16 [32, 2880], replicated, may hold values from -0.0546875 to 0.0546875
- router_bias: float32 [32], replicated, may hold values from -3 to 3
- gate_weight: bfloat16 [32, 2880, 2880], P('expert', None, 'tensor'), may hold values from -0.109375 to 0.109375
- gate_bias: float32 [32, 2880], P('expert', 'tensor'), may hold values from -6 to 6
- up_weight: bfloat16 [32, 2880, 2880], P('expert', None, 'tensor'), may hold values from -0.109375 to 0.109375
- up_bias: float32 [32, 2880], P('expert', 'tensor'), may hold values from -4 to 4
- down_weight: bfloat16 [32, 2880, 2880], P('expert', 'tensor'), may hold values from -0.078125 to 0.078125
- down_bias: float32 [32, 2880], P('expert'), may hold values from -3 to 3
- cotangent: bfloat16 [4096, 2880], P('expert'), may hold values from -6 to 6
Outputs:
- output: bfloat16 [4096, 2880], P('expert')
- input_grad: float32 [4096, 2880], P('expert')
- attn_norm_grad: float32 [2880], replicated
- q_weight_grad: float32 [4096, 2880], P('tensor', 'expert')
- q_bias_grad: float32 [4096], P('tensor')
- k_weight_grad: float32 [512, 2880], P('tensor', 'expert')
- k_bias_grad: float32 [512], P('tensor')
- v_weight_grad: float32 [512, 2880], P('tensor', 'expert')
- v_bias_grad: float32 [512], P('tensor')
- o_weight_grad: float32 [4096, 2880], P('tensor', 'expert')
- o_bias_grad: float32 [2880], replicated
- sink_logits_grad: float32 [64], P('tensor')
- moe_norm_grad: float32 [2880], replicated
- router_weight_grad: float32 [32, 2880], replicated
- router_bias_grad: float32 [32], replicated
- gate_weight_grad: float32 [32, 2880, 2880], P('expert', None, 'tensor')
- gate_bias_grad: float32 [32, 2880], P('expert', 'tensor')
- up_weight_grad: float32 [32, 2880, 2880], P('expert', None, 'tensor')
- up_bias_grad: float32 [32, 2880], P('expert', 'tensor')
- down_weight_grad: float32 [32, 2880, 2880], P('expert', 'tensor')
- down_bias_grad: float32 [32, 2880], P('expert')
The draws below stay inside these ranges and needn't reach their ends.
Inputs may be any that keep to these rules, and one draw needn't show every extreme that they name: `segment_ids`: the ids start at 0 and never fall. Each aligned run of 512 tokens holds exactly three documents, numbered on from the run before: the first ends before the run's midpoint, the last begins after it, so the middle one runs across the midpoint; the first and the last hold a fifth of 256 tokens or more (rounded down). `expert_routes`: A token names 4 different experts; among the tokens of one index of expert (256 aligned tokens) no expert is named more than 48 times.
All inputs are finite; a program needn't handle non-finite values.
Results may differ from the reference program's by a relative error of at most 0.028.
Values may be sent and summed in bfloat16 or wider, within the bound.
A program may use at most 320 MiB of HBM per device.

```python
import math
from functools import partial
import jax
import jax.numpy as jnp
import numpy as np
from jax import lax

MODEL_DIMENSION = 2880
QUERY_HEADS = 64
KEY_VALUE_HEADS = 8
HEAD_DIMENSION = 64
FF = 2880
TOP = 4
WINDOW_LENGTH = 128
ROWS = 256
LENGTH = 4096
TOKEN_TOTAL = 4096
EXPERTS = 32
CAP = 48
N_EXPERT = 16


def draw_segment_ids(key, part):
    key = jax.random.fold_in(key, 11)
    first_key, second_key = jax.random.split(key)
    run_length = 2 * ROWS
    runs = TOKEN_TOTAL // run_length
    first_cut = jax.random.randint(first_key, (runs, 1), ROWS // 5, 3 * ROWS // 4 + 1)
    second_cut = jax.random.randint(second_key, (runs, 1), 5 * ROWS // 4, 2 * ROWS - ROWS // 5 + 1)
    places = jnp.arange(run_length, dtype=jnp.int32)[None, :]
    numbers = 3 * jnp.arange(runs, dtype=jnp.int32)[:, None]
    numbers = numbers + (places >= first_cut).astype(jnp.int32) + (places >= second_cut).astype(jnp.int32)
    return numbers.reshape(TOKEN_TOTAL).astype(jnp.int32)


def level_of(rng, dims, cuts, smallest, largest):
    factor_of, own = 1.0, jax.random.fold_in(rng, 6)
    for position, shards_of in cuts:
        heights = jnp.exp(jax.random.uniform(jax.random.fold_in(own, position), (shards_of,), jnp.float32, smallest / len(cuts), largest / len(cuts)))
        factor_of = factor_of * jnp.repeat(heights, dims[position] // shards_of).reshape([-1 if axis == position else 1 for axis in range(len(dims))])
    return factor_of


def routed_block(own_key, own, number, rows, count, top, bound, skew):
    order = jax.random.permutation(own_key, count)
    heavy_load, usual = load_shares(count, rows * top, bound, skew, True), load_shares(count, rows * top, bound, skew, False)
    places = jnp.arange(count)

    def named(sizes, turn):
        used = int((sizes > 0).sum())
        fixed = max(1, used // 4)
        shifted = fixed + (places - fixed + turn * (used - fixed)) % max(1, count - fixed)
        return jnp.zeros((count,), jnp.int32).at[order[jnp.where(places < fixed, places, shifted)]].set(jnp.asarray(sizes, jnp.int32))

    sizes = jnp.where(number % 4 == 0, named(heavy_load, number // 4), named(usual, number - number // 4 - 1))
    mixed = jax.random.permutation(jax.random.fold_in(own, 3), count)
    donor, sink = mixed[0:count // 2 * 2:2], mixed[1:count // 2 * 2:2]
    slack = jnp.minimum(sizes[donor] - 1, bound - sizes[sink]) // 2
    slack = jnp.where((donor == order[0]) | (sink == order[0]) | (sizes[sink] == 0), 0, jnp.maximum(slack, 0))
    shifted = jax.random.randint(jax.random.fold_in(own, 4), (count // 2,), 0, 1 << 20) % (slack + 1)
    sizes = sizes.at[donor].add(-shifted).at[sink].add(shifted)
    labels = jnp.searchsorted(jnp.cumsum(sizes), jnp.arange(rows * top), side="right").astype(jnp.int32)
    table = labels.reshape(top, rows).T
    table = table[jax.random.permutation(jax.random.fold_in(own, 1), rows)]
    turn = jax.random.randint(jax.random.fold_in(own, 2), (rows, 1), 0, top)
    return jnp.take_along_axis(table, (jnp.arange(top)[None, :] + turn) % top, axis=1)


def load_shares(count, total, most, lean, full):
    portions = [(1 << 20) // math.isqrt(rank ** lean) + 1 for rank in range(1, count + 1)]
    largest = most if full else min(most, max(-(-total // count), total * portions[0] // sum(portions)))
    least = 1 if total - largest >= count - 1 else 0
    holding, spare = [largest] + [least] * (count - 1), total - largest - least * (count - 1)
    while spare > 0:
        candidates = [i for i in range(1, count) if holding[i] < largest] or [i for i in range(1, count) if holding[i] < most]
        whole, remaining = sum([portions[i] for i in candidates]), spare
        for i in candidates:
            more = min(most - holding[i], max(1, remaining * portions[i] // whole), spare)
            holding[i] = holding[i] + more
            spare = spare - more
    return np.array(holding)


def noise(stream_key, shape, spread, bound, cuts=(), kind=jnp.bfloat16):
    factor_of = level_of(stream_key, shape, cuts, -0.22, 0.18) if cuts else 1.0
    values = jax.random.normal(stream_key, shape, jnp.float32) * spread * factor_of
    return jnp.minimum(jnp.maximum(values, -bound), bound).astype(kind)


def setup_inputs(seed: int = 0) -> dict:
    seeds = jax.random.split(jax.random.key(seed), 24)
    layer_input = noise(seeds[0], (TOKEN_TOTAL, MODEL_DIMENSION), 1.0, 6.0, ((0, 16),))
    segment_ids = draw_segment_ids(jax.random.fold_in(seeds[23], 71), 0)
    expert_routes_keys = jax.random.split(jax.random.fold_in(seeds[2], 1), TOKEN_TOTAL // ROWS)
    expert_routes_turns = jax.random.permutation(jax.random.fold_in(seeds[2], 3), TOKEN_TOTAL // ROWS)
    expert_routes = jax.vmap(lambda own, number: routed_block(jax.random.fold_in(seeds[2], 2), own, number, ROWS, EXPERTS, TOP, CAP, 2))(expert_routes_keys, expert_routes_turns).reshape((TOKEN_TOTAL, TOP))
    attn_norm = jnp.clip(1.0 + 0.15 * jax.random.normal(seeds[3], (MODEL_DIMENSION,), jnp.float32), 0.25, 1.75)
    q_weight = noise(seeds[4], (QUERY_HEADS * HEAD_DIMENSION, MODEL_DIMENSION), MODEL_DIMENSION ** -0.5, 0.109375, ((0, 8), (1, 16)))
    q_bias = noise(seeds[5], (QUERY_HEADS * HEAD_DIMENSION,), 0.5, 3.0, ((0, 8),), jnp.float32)
    key_matrix = noise(seeds[6], (KEY_VALUE_HEADS * HEAD_DIMENSION, MODEL_DIMENSION), MODEL_DIMENSION ** -0.5, 0.109375, ((0, 8), (1, 16)))
    key_bias = noise(seeds[7], (KEY_VALUE_HEADS * HEAD_DIMENSION,), 0.5, 3.0, ((0, 8),), jnp.float32)
    value_matrix = noise(seeds[8], (KEY_VALUE_HEADS * HEAD_DIMENSION, MODEL_DIMENSION), MODEL_DIMENSION ** -0.5, 0.109375, ((0, 8), (1, 16)))
    value_bias = noise(seeds[9], (KEY_VALUE_HEADS * HEAD_DIMENSION,), 0.3, 3.0, ((0, 8),), jnp.float32)
    o_weight = noise(seeds[10], (QUERY_HEADS * HEAD_DIMENSION, MODEL_DIMENSION), (QUERY_HEADS * HEAD_DIMENSION // 32) ** -0.5, 0.5, ((0, 8), (1, 16)))
    o_bias = noise(seeds[11], (MODEL_DIMENSION,), 0.3, 3.0, (), jnp.float32)
    sink_scores = noise(seeds[12], (QUERY_HEADS,), 1.0, 3.0, ((0, 8),), jnp.float32)
    moe_norm = jnp.clip(1.0 + 0.15 * jax.random.normal(seeds[13], (MODEL_DIMENSION,), jnp.float32), 0.25, 1.75)
    router_weight = noise(seeds[14], (EXPERTS, MODEL_DIMENSION), (4 * MODEL_DIMENSION) ** -0.5, 0.0546875)
    router_bias = noise(seeds[15], (EXPERTS,), 0.3, 3.0, (), jnp.float32)
    gate_weight = noise(seeds[16], (EXPERTS, MODEL_DIMENSION, FF), MODEL_DIMENSION ** -0.5, 0.109375, ((0, 16), (2, 8)))
    gate_bias = noise(seeds[17], (EXPERTS, FF), 2.0, 6.0, ((0, 16), (1, 8)), jnp.float32)
    up_weight = noise(seeds[18], (EXPERTS, MODEL_DIMENSION, FF), MODEL_DIMENSION ** -0.5, 0.109375, ((0, 16), (2, 8)))
    up_bias = noise(seeds[19], (EXPERTS, FF), 1.0, 4.0, ((0, 16), (1, 8)), jnp.float32)
    down_weight = noise(seeds[20], (EXPERTS, FF, MODEL_DIMENSION), (2 * FF) ** -0.5, 0.078125, ((0, 16), (1, 8)))
    down_bias = noise(seeds[21], (EXPERTS, MODEL_DIMENSION), 0.2, 3.0, ((0, 16),), jnp.float32)
    cotangent = noise(seeds[22], (TOKEN_TOTAL, MODEL_DIMENSION), 1.0, 6.0, ((0, 16),))
    return {"layer_input": layer_input, "segment_ids": segment_ids, "expert_routes": expert_routes, "attn_norm": attn_norm, "q_weight": q_weight, "q_bias": q_bias, "key_matrix": key_matrix, "key_bias": key_bias, "value_matrix": value_matrix, "value_bias": value_bias, "o_weight": o_weight, "o_bias": o_bias, "sink_scores": sink_scores, "moe_norm": moe_norm, "router_weight": router_weight, "router_bias": router_bias, "gate_weight": gate_weight, "gate_bias": gate_bias, "up_weight": up_weight, "up_bias": up_bias, "down_weight": down_weight, "down_bias": down_bias, "cotangent": cotangent}


@jax.custom_vjp
def reduced_precision(v):
    return lax.optimization_barrier(v.astype(jnp.bfloat16)).astype(jnp.float32)

@jax.custom_vjp
def low_back(v):
    return v

def low_keep(v):
    return (reduced_precision(v), None)

def low_pass(kept, grad):
    return (grad,)

def back_keep(v):
    return (v, None)

def back_low(kept, grad):
    return (reduced_precision(grad),)
reduced_precision.defvjp(low_keep, low_pass)
low_back.defvjp(back_keep, back_low)
EPSILON = 1e-05
NEGATIVE = -1e+30
ROPE_BASE = 150000.0
HIGHEST_PRECISION = lax.Precision.HIGHEST

def rms_normal(values):
    return values * lax.rsqrt(lax.optimization_barrier(jnp.mean(values * values, axis=-1, keepdims=True)) + EPSILON)

def apply_rotary(values, cosine_lookup, sine_lookup):
    half_size = values.shape[-1] // 2
    first_half = values[..., :half_size]
    second_half = values[..., half_size:]
    return jnp.concatenate([first_half * cosine_lookup - second_half * sine_lookup, second_half * cosine_lookup + first_half * sine_lookup], axis=-1)

def clamped_swiglu(gate_pre, up_pre):
    gate_soft = 7.0 - jax.nn.softplus(7.0 - gate_pre)
    up_soft = 7.0 * jnp.tanh(up_pre / 7.0)
    return (up_soft + 1.0) * gate_soft * jax.nn.sigmoid(1.702 * gate_soft)

def slot_numbers(routes_block, expert_count):
    flat_routes = routes_block.reshape(-1)
    onehot_marks = (flat_routes[:, None] == jnp.arange(expert_count, dtype=jnp.int32)[None, :]).astype(jnp.int32)
    before = jnp.cumsum(onehot_marks, axis=0) - onehot_marks
    return (flat_routes, lax.optimization_barrier(jnp.sum(onehot_marks * before, axis=1)))

def expert_apply(pieces):
    expert_rows, gate_w, gate_b, up_w, up_b, down_w, down_b = pieces
    gate_pre = low_back(jnp.dot(expert_rows, gate_w, precision=HIGHEST_PRECISION) + gate_b)
    up_pre = low_back(jnp.dot(expert_rows, up_w, precision=HIGHEST_PRECISION) + up_b)
    hidden = reduced_precision(clamped_swiglu(gate_pre, up_pre))
    return low_back(jnp.dot(hidden, down_w, precision=HIGHEST_PRECISION) + down_b)

def forward_pass(layer_input, attn_norm, q_weight, q_bias, key_matrix, key_bias, value_matrix, value_bias, o_weight, o_bias, sink_scores, moe_norm, router_weight, router_bias, gate_weight, gate_bias, up_weight, up_bias, down_weight, down_bias, segment_ids, expert_routes):
    score_scale = HEAD_DIMENSION ** (-0.5)
    query_group_count = QUERY_HEADS // KEY_VALUE_HEADS
    block_length = 2 * ROWS
    normal_one = rms_normal(layer_input)
    normed = reduced_precision(normal_one * attn_norm)
    query_pre = low_back(jnp.dot(normed, q_weight.T, precision=HIGHEST_PRECISION) + q_bias)
    key_before_rotary = low_back(jnp.dot(normed, key_matrix.T, precision=HIGHEST_PRECISION) + key_bias)
    value_projected = low_back(jnp.dot(normed, value_matrix.T, precision=HIGHEST_PRECISION) + value_bias)
    frequencies = ROPE_BASE ** (-(2.0 * jnp.arange(HEAD_DIMENSION // 2, dtype=jnp.float32)) / HEAD_DIMENSION)
    token_places = jnp.arange(TOKEN_TOTAL, dtype=jnp.int32) % LENGTH
    angles = token_places.astype(jnp.float32)[:, None] * frequencies[None, :]
    cosine_lookup = jnp.cos(angles)[:, None, :]
    sine_lookup = jnp.sin(angles)[:, None, :]
    query_rotated = reduced_precision(apply_rotary(query_pre.reshape(TOKEN_TOTAL, QUERY_HEADS, HEAD_DIMENSION), cosine_lookup, sine_lookup))
    key_rotated = reduced_precision(apply_rotary(key_before_rotary.reshape(TOKEN_TOTAL, KEY_VALUE_HEADS, HEAD_DIMENSION), cosine_lookup, sine_lookup))
    value_reduced = reduced_precision(value_projected.reshape(TOKEN_TOTAL, KEY_VALUE_HEADS, HEAD_DIMENSION))
    grouped_heads = query_rotated.reshape(TOKEN_TOTAL, KEY_VALUE_HEADS, query_group_count, HEAD_DIMENSION)
    key_with_padding = jnp.concatenate([jnp.zeros((WINDOW_LENGTH, KEY_VALUE_HEADS, HEAD_DIMENSION), jnp.float32), key_rotated], axis=0)
    value_with_padding = jnp.concatenate([jnp.zeros((WINDOW_LENGTH, KEY_VALUE_HEADS, HEAD_DIMENSION), jnp.float32), value_reduced], axis=0)
    segment_padded = jnp.concatenate([jnp.full((WINDOW_LENGTH,), -1, jnp.int32), segment_ids.astype(jnp.int32)])
    sink_per_query = sink_scores.reshape(KEY_VALUE_HEADS, query_group_count)
    block_count = TOKEN_TOTAL // block_length

    def one_block(block):
        start = (block * block_length).astype(jnp.int32)
        query_block = lax.dynamic_slice_in_dim(grouped_heads, start, block_length)
        key_block = lax.dynamic_slice_in_dim(key_with_padding, start, WINDOW_LENGTH + block_length)
        value_block = lax.dynamic_slice_in_dim(value_with_padding, start, WINDOW_LENGTH + block_length)
        query_segments = lax.dynamic_slice_in_dim(segment_padded, start + WINDOW_LENGTH, block_length)
        key_segments = lax.dynamic_slice_in_dim(segment_padded, start, WINDOW_LENGTH + block_length)
        query_places = jnp.arange(block_length, dtype=jnp.int32) + WINDOW_LENGTH
        key_places = jnp.arange(WINDOW_LENGTH + block_length, dtype=jnp.int32)
        distance = query_places[:, None] - key_places[None, :]
        allowed = (distance >= 0) & (distance < WINDOW_LENGTH) & (query_segments[:, None] == key_segments[None, :])
        raw_scores = jnp.einsum('qhgd,khd->hgqk', query_block, key_block, precision=HIGHEST_PRECISION) * score_scale
        raw_scores = low_back(raw_scores)
        masked = jnp.where(allowed[None, None], raw_scores, NEGATIVE)
        row_top = jnp.maximum(lax.optimization_barrier(jnp.max(masked, axis=-1)), sink_per_query[:, :, None])
        weights_exp = jnp.exp(masked - row_top[..., None])
        row_total = lax.optimization_barrier(jnp.sum(weights_exp, axis=-1)) + jnp.exp(sink_per_query[:, :, None] - row_top)
        probs = reduced_precision(weights_exp / row_total[..., None])
        return jnp.einsum('hgqk,khd->qhgd', probs, value_block, precision=HIGHEST_PRECISION)
    attended = lax.map(jax.checkpoint(one_block), jnp.arange(block_count, dtype=jnp.int32))
    attn_low = reduced_precision(low_back(attended.reshape(TOKEN_TOTAL, QUERY_HEADS * HEAD_DIMENSION)))
    attn_out = low_back(jnp.dot(attn_low, o_weight, precision=HIGHEST_PRECISION))
    middle = layer_input + attn_out + o_bias
    normal_two = rms_normal(middle)
    moe_in = reduced_precision(normal_two * moe_norm)
    logits = jnp.dot(moe_in, router_weight.T, precision=HIGHEST_PRECISION) + router_bias
    route_marks = (expert_routes[:, :, None] == jnp.arange(EXPERTS, dtype=jnp.int32)[None, None, :]).astype(jnp.float32)
    chosen = lax.optimization_barrier(jnp.sum(route_marks * logits[:, None, :], axis=2))
    gate_probs = jax.nn.softmax(chosen, axis=1)
    flat_expert, slot_index = jax.vmap(partial(slot_numbers, expert_count=EXPERTS))(expert_routes.reshape(N_EXPERT, ROWS, TOP))
    group_ids = jnp.arange(N_EXPERT, dtype=jnp.int32)[:, None]
    sources = jnp.repeat(moe_in.reshape(N_EXPERT, ROWS, MODEL_DIMENSION), TOP, axis=1)
    slot_buffer = jnp.zeros((N_EXPERT, EXPERTS, CAP, MODEL_DIMENSION), jnp.float32).at[group_ids, flat_expert, slot_index].set(sources)
    expert_rows = slot_buffer.transpose(1, 0, 2, 3).reshape(EXPERTS, N_EXPERT * CAP, MODEL_DIMENSION)
    produced = lax.map(jax.checkpoint(expert_apply), (expert_rows, gate_weight, gate_bias, up_weight, up_bias, down_weight, down_bias))
    returned = produced.reshape(EXPERTS, N_EXPERT, CAP, MODEL_DIMENSION).transpose(1, 0, 2, 3)
    picked = returned[group_ids, flat_expert, slot_index].reshape(TOKEN_TOTAL, TOP, MODEL_DIMENSION)
    moe_out = lax.optimization_barrier(jnp.sum(gate_probs[:, :, None] * picked, axis=1))
    return middle + moe_out

def reference(layer_input, segment_ids, expert_routes, attn_norm, q_weight, q_bias, key_matrix, key_bias, value_matrix, value_bias, o_weight, o_bias, sink_scores, moe_norm, router_weight, router_bias, gate_weight, gate_bias, up_weight, up_bias, down_weight, down_bias, cotangent):
    floats = tuple((array_in.astype(jnp.float32) for array_in in (layer_input, attn_norm, q_weight, q_bias, key_matrix, key_bias, value_matrix, value_bias, o_weight, o_bias, sink_scores, moe_norm, router_weight, router_bias, gate_weight, gate_bias, up_weight, up_bias, down_weight, down_bias)))
    function = partial(forward_pass, segment_ids=segment_ids, expert_routes=expert_routes)
    result, pullback = jax.vjp(function, *floats)
    grads = pullback(cotangent.astype(jnp.float32))
    return (result.astype(jnp.bfloat16), grads[0], grads[1], grads[2], grads[3], grads[4], grads[5], grads[6], grads[7], grads[8], grads[9], grads[10], grads[11], grads[12], grads[13], grads[14], grads[15], grads[16], grads[17], grads[18], grads[19])
```

```python
import functools

import jax
import jax.numpy as jnp
from jax import lax
from jax.experimental import pallas as pl
from jax.experimental.pallas import tpu as pltpu
from jax.sharding import PartitionSpec as P

HEAD_DIMENSION = 64
TOP = 4
WINDOW_LENGTH = 128
SLOTS = 48
SIDE = 4
MODEL = 2880
WIDTH = 2944
EDGE = WIDTH - 128
HIDDEN = 360
LANES = 384
SHARD_ROWS = 192
HALF_ROWS = 8 * SLOTS

EPSILON = 1e-05
NEGATIVE = -1e30
ROPE_BASE = 150000.0
HIGHEST_PRECISION = lax.Precision.HIGHEST
MESH = pl.DeviceIdType.MESH
MIB = 1024 * 1024
VMEM = pltpu.VMEM
DMA = pltpu.SemaphoreType.DMA
ANYWHERE = pl.BlockSpec(memory_space=pl.ANY)
INSIDE = pl.BlockSpec(memory_space=pltpu.VMEM)
COLUMNS = tuple((start, min(512, WIDTH - start)) for start in range(0, WIDTH, 512))


def place():
    expert_index = lax.axis_index("expert")
    tensor_index = lax.axis_index("tensor")
    return (
        lax.div(expert_index, SIDE),
        lax.rem(expert_index, SIDE),
        lax.div(tensor_index, 2),
        lax.rem(tensor_index, 2),
    )


def around(position, by):
    return lax.rem(position + by + SIDE, SIDE)


def offset(group_x, group_core, turn):
    step_z = 2 * turn + group_core
    return step_z, lax.rem(step_z - group_x + SIDE, SIDE)


def slot_of(group_x, group_core, turn):
    return group_core * 8 + group_x * 2 + turn


def remote(src, dst, send_sem, recv_sem, device):
    return pltpu.make_async_remote_copy(
        src_ref=src,
        dst_ref=dst,
        send_sem=send_sem,
        recv_sem=recv_sem,
        device_id=device,
        device_id_type=MESH,
    )


def greet(barrier, device):
    pl.semaphore_signal(barrier, inc=1, device_id=device, device_id_type=MESH)


def in_turns(*running):
    running = list(running)
    while running:
        for one in list(running):
            if next(one, "end") == "end":
                running.remove(one)


def merged_tail(total):
    lane = lax.broadcasted_iota(jnp.int32, total.shape, 1)
    whole = total + pltpu.roll(total, 96, 1)
    high = whole.astype(jnp.bfloat16).astype(jnp.float32)
    low = pltpu.roll(whole - high, 32, 1)
    return jnp.where(lane < 64, total, jnp.where(lane < 96, high, low))


def add_into(dst, sources, rows):
    def step(i, carry):
        at = pl.ds(pl.multiple_of(i * 16, 16), 16)
        total = sources[0][at, :].astype(jnp.float32)
        for source in sources[1:]:
            total = total + source[at, :].astype(jnp.float32)
        dst[at, :EDGE] = total[:, :EDGE].astype(jnp.bfloat16)
        dst[at, EDGE:] = merged_tail(total[:, EDGE:]).astype(jnp.bfloat16)
        return carry

    lax.fori_loop(0, rows // 16, step, 0)


def tensor_sum_steps(rows, part, out, from_core, sums, from_chip, sem):
    z, y, x, c = place()
    e = z * SIDE + y
    me = 2 * x + c
    sibling = (e, 2 * x + 1 - c)

    def swap(r):
        return remote(
            part.at[2 * around(x, r) + 1 - c], from_core.at[r],
            sem.at[0, r], sem.at[1, r], sibling,
        )

    def give(r):
        return remote(
            sums.at[r], from_chip.at[r], sem.at[2, r], sem.at[3, r],
            (e, 2 * around(x, r) + c),
        )

    def spread(r):
        return remote(
            out.at[me], out.at[me], sem.at[4, r], sem.at[5, r],
            (e, 2 * around(x, r) + c),
        )

    def arrives(r):
        there = out.at[2 * around(x, -r) + c]
        return remote(there, there, sem.at[4, r], sem.at[5, r], sibling)

    def pass_on(r):
        block = out.at[2 * around(x, -r) + c]
        return remote(block, block, sem.at[6, r], sem.at[7, r], sibling)

    def passed(r):
        block = out.at[2 * around(x, -r) + 1 - c]
        return remote(block, block, sem.at[6, r], sem.at[7, r], sibling)

    order = (2, 1, 3, 0)
    for r in order:
        swap(r).start()
    yield
    for r in order[:3]:
        swap(r).wait_recv()
        add_into(sums.at[r], (part.at[2 * around(x, r) + c], from_core.at[r]), rows)
        give(r).start()
    swap(0).wait_recv()
    yield
    for r in (1, 3, 2):
        give(r).wait_recv()
    add_into(
        out.at[me],
        (part.at[me], from_core.at[0], from_chip.at[1], from_chip.at[2], from_chip.at[3]),
        rows,
    )
    for r in (2, 1, 3):
        spread(r).start()
    pass_on(0).start()
    yield
    for r in (1, 3, 2):
        arrives(r).wait_recv()
        pass_on(r).start()
    yield
    for r in range(4):
        passed(r).wait_recv()
        swap(r).wait_send()
        pass_on(r).wait_send()
    for r in (1, 2, 3):
        give(r).wait_send()
        spread(r).wait_send()


def tensor_sum_scratch(rows):
    block = (SIDE, rows, WIDTH)
    return [VMEM(block, jnp.bfloat16)] * 3 + [DMA((8, 4))]


class Legs:
    def __init__(self, sign):
        z, y, x, c = place()
        self.z, self.y, self.x, self.c = z, y, x, c
        self.e, self.t = z * SIDE + y, 2 * x + c
        self.sibling = (self.e, 2 * x + 1 - c)
        self.beside = tuple((self.e, 2 * around(x, by) + c) for by in (-1, 1))
        self.there, self.back, self.own, self.slot = [], [], [], []
        for k in range(4):
            a, i = divmod(k, 2)
            gx = around(x, 2 * a)
            dz, dy = offset(gx, c, i)
            ahead = (around(z, dz) * SIDE + around(y, dy), self.t)
            behind = (around(z, -dz) * SIDE + around(y, -dy), self.t)
            self.there.append(ahead if sign > 0 else behind)
            self.back.append(behind if sign > 0 else ahead)
            self.own.append(jnp.logical_and(gx == 0, c == 0) if i == 0 else None)
            self.slot.append(slot_of(gx, c, i))

    def greet(self, barrier):
        greet(barrier, self.sibling)
        greet(barrier, self.beside[0])
        greet(barrier, self.beside[1])
        count = jnp.int32(11)
        for k in range(4):
            def both(k=k):
                greet(barrier, self.there[k])
                greet(barrier, self.back[k])

            self.either(k, lambda: None, both)
            if self.own[k] is not None:
                count = count - 2 * self.own[k].astype(jnp.int32)
        return count

    def either(self, k, at_home, away):
        own = self.own[k]
        if own is None:
            away()
        else:
            pl.when(own)(at_home)
            pl.when(jnp.logical_not(own))(away)


class Dispatch:
    def __init__(self, legs, blocks, out, j, yz, side, core, at_home=False):
        self.legs, self.blocks, self.out, self.j = legs, blocks, out, j
        self.yz, self.side, self.core, self.at_home = yz, side, core, at_home

    def leg(self, k):
        j = self.j
        return remote(
            self.blocks.at[k, j], self.out.at[j, self.legs.slot[k]],
            self.yz.at[0, j, k], self.yz.at[1, j, k], self.legs.there[k],
        )

    def kept(self, k):
        j = self.j
        return pltpu.make_async_copy(
            self.blocks.at[k, j], self.out.at[j, self.legs.slot[k]], self.yz.at[1, j, k]
        )

    def block_copy(self, gx, gc, i, sems, n, device, own=None):
        block = self.out.at[self.j, slot_of(gx, gc, i)]
        src = self.blocks.at[own, self.j] if self.at_home and own is not None else block
        return remote(src, block, sems.at[0, self.j, n], sems.at[1, self.j, n], device)

    def aside(self, direction, i):
        legs = self.legs
        return self.block_copy(
            legs.x, legs.c, i, self.side, 2 * direction + i, legs.beside[direction], i
        )

    def from_side(self, direction, i):
        legs = self.legs
        return self.block_copy(
            around(legs.x, 1 - 2 * direction), legs.c, i,
            self.side, 2 * direction + i, legs.beside[direction],
        )

    def across(self, r, i):
        legs = self.legs
        return self.block_copy(
            around(legs.x, r), legs.c, i, self.core, 2 * r + i, legs.sibling,
            r + i if r in (0, 2) else None,
        )

    def from_core(self, r, i):
        legs = self.legs
        return self.block_copy(
            around(legs.x, r), 1 - legs.c, i, self.core, 2 * r + i, legs.sibling
        )

    def start(self, k):
        if self.at_home:
            self.kept(k).start()
        else:
            self.legs.either(k, lambda: self.kept(k).start(), lambda: self.leg(k).start())

    def landed(self, k):
        if self.at_home:
            self.kept(k).wait()
        else:
            self.legs.either(k, lambda: self.kept(k).wait(), lambda: self.leg(k).wait_recv())

    def steps(self):
        for k in range(4):
            self.start(k)
        yield
        for i in (0, 1):
            self.landed(i)
            self.aside(0, i).start()
            self.aside(1, i).start()
            self.across(0, i).start()
            yield
        for i in (0, 1):
            self.landed(2 + i)
            self.across(2, i).start()
            yield
        for i in (0, 1):
            for direction in (0, 1):
                self.from_side(direction, i).wait_recv()
                self.across(1 if direction == 0 else 3, i).start()
            yield

    def pass_on(self):
        for k in range(4):
            self.start(k)
        for i in (0, 1):
            self.aside(0, i).start()
            self.aside(1, i).start()
        for r in (0, 2):
            for i in (0, 1):
                self.across(r, i).start()

    def from_sides(self):
        for i in (0, 1):
            for direction in (0, 1):
                self.from_side(direction, i).wait_recv()
                self.across(1 if direction == 0 else 3, i).start()

    def rest(self):
        if self.at_home:
            for k in range(4):
                self.landed(k)
        for r in range(4):
            for i in (0, 1):
                self.from_core(r, i).wait_recv()

    def sent(self):
        for r in range(4):
            for i in (0, 1):
                self.across(r, i).wait_send()
        for direction in (0, 1):
            for i in (0, 1):
                self.aside(direction, i).wait_send()
        if not self.at_home:
            for k in range(4):
                self.legs.either(k, lambda: None, lambda k=k: self.leg(k).wait_send())


DISPATCH_SEMS = [DMA((2, 2, 4)), DMA((2, 2, 4)), DMA((2, 2, 8))]


def own_experts():
    z, y, x, c = place()
    found = []
    for a in (0, 1):
        for i in (0, 1):
            dz, dy = offset(around(x, 2 * a), c, i)
            block = around(z, dz) * SIDE + around(y, dy)
            found += [2 * block, 2 * block + 1]
    return found


def expert_rows(shape, first_lane):
    row = lax.broadcasted_iota(jnp.int32, shape, 0)
    lane = lax.broadcasted_iota(jnp.int32, shape, 1) - first_lane
    found = jnp.full(shape, -1, jnp.int32)
    for b, expert in enumerate(own_experts()):
        found = jnp.where(row == b, expert, found)
    return (lane == found).astype(jnp.float32)


def fill_slots(slots, own_rank):
    for b in range(8):
        place_of = lax.broadcasted_iota(jnp.int32, (SLOTS, own_rank.shape[1]), 0)
        hit = own_rank[b : b + 1, :] == place_of.astype(jnp.float32)
        slots[b * SLOTS : (b + 1) * SLOTS, :] = hit.astype(jnp.float32).astype(jnp.bfloat16)


class Gather:
    def __init__(self, shard, out, own_sem, send, recv):
        z, y, x, c = place()
        self.z, self.y, self.t = z, y, 2 * x + c
        self.shard, self.out, self.own_sem, self.send, self.recv = shard, out, own_sem, send, recv

    def at(self, axis, by, other):
        if axis == 0:
            return around(self.z, by) * SIDE + around(self.y, other)
        return around(self.z, other) * SIDE + around(self.y, by)

    def partners(self):
        return [(self.at(axis, by, 0), self.t) for axis in (0, 1) for by in (1, -1)]

    def ring(self, h, n, axis, item):
        half = SHARD_ROWS // 2
        quarter = half // 2
        first = item == 0
        out, send, recv, at = self.out, self.send, self.recv, self.at

        def rows(start, size):
            return pl.ds(h * half + start, size)

        def to(k):
            return (at(axis, (1, -1)[k], 0), self.t)

        def whole(k):
            index = at(axis, 0, item)
            src = self.shard.at[rows(0, half)] if first else out.at[index, rows(0, half)]
            return remote(
                src, out.at[index, rows(0, half)], send.at[h, n, k], recv.at[h, n, k], to(k)
            )

        def whole_in(k):
            there = out.at[at(axis, (-1, 1)[k], item), rows(0, half)]
            return remote(there, there, send.at[h, n, k], recv.at[h, n, k], to(k))

        def onward(k):
            there = out.at[at(axis, (-1, 1)[k], item), rows(k * quarter, quarter)]
            return remote(there, there, send.at[h, n, 2 + k], recv.at[h, n, 2 + k], to(k))

        def onward_in(k):
            there = out.at[at(axis, 2, item), rows(k * quarter, quarter)]
            return remote(there, there, send.at[h, n, 2 + k], recv.at[h, n, 2 + k], to(k))

        return whole, whole_in, onward, onward_in

    def steps(self):
        own = pltpu.make_async_copy(self.shard, self.out.at[self.at(0, 0, 0)], self.own_sem)
        own.start()
        first = [self.ring(h, 0, 1 - h, 0) for h in (0, 1)]
        second = [
            {item: self.ring(h, 1 + item % 4, h, item) for item in (0, -1, 1, 2)} for h in (0, 1)
        ]
        for h in (0, 1):
            for k in (0, 1):
                first[h][0](k).start()
        for h in (0, 1):
            for k in (0, 1):
                second[h][0][0](k).start()
        yield
        for k in (0, 1):
            for h in (0, 1):
                first[h][1](k).wait_recv()
                first[h][2](k).start()
                for direction in (0, 1):
                    second[h][(-1, 1)[k]][0](direction).start()
        for k in (0, 1):
            for h in (0, 1):
                second[h][0][1](k).wait_recv()
                second[h][0][2](k).start()
        yield
        for h in (0, 1):
            for k in (0, 1):
                first[h][3](k).wait_recv()
            for k in (0, 1):
                second[h][2][0](k).start()
        yield
        for item in (-1, 1, 2):
            for k in (0, 1):
                for h in (0, 1):
                    second[h][item][1](k).wait_recv()
                    second[h][item][2](k).start()
            yield
        own.wait()
        for h in (0, 1):
            for item in (0, -1, 1, 2):
                for k in (0, 1):
                    second[h][item][3](k).wait_recv()
            for steps in (first[h], *second[h].values()):
                for k in (0, 1):
                    steps[0](k).wait_send()
                    steps[2](k).wait_send()


def experts_kernel(
    own_rank, own_gates, rows, grad_blocks, gate_weight, up_weight, down_weight, gate_bias, up_bias,
    down_bias, parts, kept_rows, kept_hidden, kept_grads, grads,
    bias, blocks, slots, table, stage, both, down, grad_stage, raw, pre,
    hidden, weighed, grad_low, made,
    yz, side, core, grad_home, grad_side, grad_core, load_sem, grad_sem, keep_sem, made_sem,
):
    legs = Legs(1)
    barrier = pltpu.get_barrier_semaphore()
    count = legs.greet(barrier)
    dispatch = [Dispatch(legs, blocks, table, j, yz, side, core) for j in (0, 1)]
    relay = [
        Dispatch(legs, grad_blocks, grads, j, grad_home, grad_side, grad_core, at_home=True)
        for j in (0, 1)
    ]
    all_rows = 2 * HALF_ROWS

    def load(j, n):
        source = (gate_weight, up_weight, down_weight)[n]
        return pltpu.make_async_copy(source.at[j], stage.at[n], load_sem.at[n])

    def grad_load(n):
        j, half = divmod(n, 2)
        return pltpu.make_async_copy(
            grads.at[j, pl.ds(half * 8, 8)], grad_stage.at[n % 2], grad_sem.at[n % 2]
        )

    for n in range(3):
        load(0, n).start()
    bias[...] = jnp.zeros_like(bias)
    for j in (0, 1):
        bias[j, :, :HIDDEN] = gate_bias[j : j + 1, :]
        bias[j, :, LANES : LANES + HIDDEN] = up_bias[j : j + 1, :]
    bias_share = jnp.where(legs.t == 0, 1.0, 0.0)

    def bias_rows(j, at, size):
        whole = down_bias[j : j + 1, at] * bias_share
        high = whole.astype(jnp.bfloat16).astype(jnp.float32)
        row = lax.broadcasted_iota(jnp.int32, (LANES - HIDDEN, size), 0)
        return jnp.where(row == 0, high, jnp.where(row == 1, whole - high, 0.0))

    fill_slots(slots, own_rank)
    marks_of = slots[...]
    for start, size in COLUMNS:
        made_rows = jnp.dot(
            marks_of, rows[:, start : start + size], preferred_element_type=jnp.float32
        )
        blocks[:, :, :, start : start + size] = made_rows.astype(jnp.bfloat16).reshape(
            4, 2, SLOTS, size
        )
    for b in range(8):
        marks_b = slots[b * SLOTS : (b + 1) * SLOTS, :].astype(jnp.float32)
        gates = jnp.sum(marks_b * own_gates[b : b + 1, :], axis=1, keepdims=True)
        lane = lax.broadcasted_iota(jnp.int32, (SLOTS, 128), 1)
        high = gates.astype(jnp.bfloat16).astype(jnp.float32)
        middle = (gates - high).astype(jnp.bfloat16).astype(jnp.float32)
        low = gates - high - middle
        edge = blocks[b // 2, b % 2, :, EDGE:].astype(jnp.float32)
        edge = jnp.where(
            lane == 64, high, jnp.where(lane == 65, middle, jnp.where(lane == 66, low, edge))
        )
        blocks[b // 2, b % 2, :, EDGE:] = edge.astype(jnp.bfloat16)
    pl.semaphore_wait(barrier, count)

    def fill(j):
        for n in range(3):
            load(j, n).wait()

        def copy_lanes(i, carry):
            at = pl.ds(pl.multiple_of(i * 128, 128), 128)
            blank = jnp.zeros((LANES - HIDDEN, 128), jnp.float32)
            for n in range(3):
                under = bias_rows(j, at, 128) if n == 2 else blank
                values = jnp.concatenate([stage[n, :, at].astype(jnp.float32), under], axis=0)
                values = values.astype(jnp.bfloat16)
                if n == 2:
                    down[j, :, at] = values
                else:
                    both[j, n * LANES : (n + 1) * LANES, at] = values
            return carry

        lax.fori_loop(0, EDGE // 128, copy_lanes, 0)
        both[j, :, EDGE:] = jnp.zeros((2 * LANES, 128), jnp.bfloat16)
        down[j, :, EDGE:] = jnp.zeros((LANES, 128), jnp.bfloat16)
        blank = jnp.zeros((LANES - HIDDEN, MODEL - EDGE), jnp.float32)
        for n in range(3):
            under = bias_rows(j, slice(EDGE, MODEL), MODEL - EDGE) if n == 2 else blank
            values = jnp.concatenate([stage[n, :, EDGE:].astype(jnp.float32), under], axis=0)
            values = values.astype(jnp.bfloat16)
            if n == 2:
                down[j, :, EDGE:MODEL] = values
            else:
                both[j, n * LANES : (n + 1) * LANES, EDGE:MODEL] = values
        if j == 0:
            for n in range(3):
                load(1, n).start()

    def raw_grads(j):
        relay[j].rest()
        grad_load(2 * j).start()
        grad_load(2 * j + 1).start()
        for half in (0, 1):
            grad_load(2 * j + half).wait()
            raw[j, half * HALF_ROWS : (half + 1) * HALF_ROWS] = lax.dot_general(
                grad_stage[half].reshape(HALF_ROWS, WIDTH), down[j],
                (((1,), (1,)), ((), ())), preferred_element_type=jnp.float32,
            )

    first, second = dispatch[0].steps(), dispatch[1].steps()

    def advance(steps, count):
        for _ in range(count):
            next(steps)

    advance(first, 1)
    fill(0)
    advance(first, 2)
    advance(second, 1)
    advance(first, 2)
    fill(1)
    advance(second, 2)
    advance(first, 2)
    dispatch[0].rest()

    def keep_rows(j):
        return pltpu.make_async_copy(table.at[j], kept_rows.at[j], keep_sem.at[j])

    def keep(j):
        return (
            pltpu.make_async_copy(made.at[0], parts.at[0, j], made_sem.at[0]),
            pltpu.make_async_copy(made.at[1], parts.at[1, j], made_sem.at[1]),
            pltpu.make_async_copy(weighed.at[j], kept_hidden.at[j], made_sem.at[2 + 2 * j]),
            pltpu.make_async_copy(grad_low.at[j], kept_grads.at[j], made_sem.at[3 + 2 * j]),
        )

    def inner_products(j):
        pre[j] = (
            lax.dot_general(
                table[j].reshape(all_rows, WIDTH), both[j],
                (((1,), (1,)), ((), ())), preferred_element_type=jnp.float32,
            )
            + bias[j]
        )

    def gates_of(j, i):
        edge = table[
            j, lax.div(i, 3), pl.ds(pl.multiple_of(lax.rem(i, 3) * 16, 16), 16), EDGE:
        ].astype(jnp.float32)
        edge_lane = lax.broadcasted_iota(jnp.int32, (16, 128), 1)
        return jnp.sum(
            jnp.where((edge_lane >= 64) & (edge_lane < 67), edge, 0.0), axis=1, keepdims=True
        )

    def soft_gate(gate_pre):
        above = 7.0 - gate_pre
        small = jnp.exp(-jnp.abs(above))
        gate_soft = 7.0 - (jnp.maximum(above, 0.0) + jnp.log1p(small))
        open_part = jnp.where(above >= 0.0, 1.0, small) / (1.0 + small)
        return gate_soft, open_part

    def activations(j):
        def activate(i, at):
            lane = lax.broadcasted_iota(jnp.int32, (16, LANES), 1)
            gates = gates_of(j, i)
            gate_soft, _ = soft_gate(pre[j, at, :LANES])
            up_one = 7.0 * jnp.tanh(pre[j, at, LANES:] * (1.0 / 7.0)) + 1.0
            value = up_one * gate_soft * jax.nn.sigmoid(1.702 * gate_soft)
            value = value.astype(jnp.bfloat16).astype(jnp.float32)
            value = jnp.where(lane < HIDDEN, value, jnp.where(lane < HIDDEN + 2, 1.0, 0.0))
            gates_high = gates.astype(jnp.bfloat16).astype(jnp.float32)
            hidden[j, at, :] = value.astype(jnp.bfloat16)
            weighed[j, at, :] = jnp.where(
                lane == HIDDEN + 1, gates - gates_high, value * gates
            ).astype(jnp.bfloat16)

        over_rows(activate, all_rows)

    def activation_grads(j):
        def activate(i, at):
            gates = gates_of(j, i)
            raw_grad = raw[j, at, :]
            gate_soft, open_part = soft_gate(pre[j, at, :LANES])
            up_tanh = jnp.tanh(pre[j, at, LANES:] * (1.0 / 7.0))
            up_one = 7.0 * up_tanh + 1.0
            sig = jax.nn.sigmoid(1.702 * gate_soft)
            through = gate_soft * sig
            gate_grad = jnp.sum(
                hidden[j, at, :].astype(jnp.float32) * raw_grad, axis=1, keepdims=True
            )
            hidden_grad = gates * raw_grad
            grad_low[j, at, :LANES] = (
                hidden_grad * up_one * (sig + 1.702 * through * (1.0 - sig)) * open_part
            ).astype(jnp.bfloat16)
            grad_low[j, at, LANES:] = (
                hidden_grad * through * (1.0 - up_tanh * up_tanh)
            ).astype(jnp.bfloat16)
            high = gate_grad.astype(jnp.bfloat16).astype(jnp.float32)
            lane = lax.broadcasted_iota(jnp.int32, (16, 128), 1)
            pre[j, at, :128] = jnp.where(
                lane == 64, high, jnp.where(lane == 96, gate_grad - high, 0.0)
            )

        over_rows(activate, all_rows)

    def row_grads(j, columns):
        for start, size in columns:
            row_grad = jnp.dot(
                grad_low[j], both[j, :, start : start + size], preferred_element_type=jnp.float32
            )
            if start + size == WIDTH:
                edge = row_grad[:, size - 128 :] + pre[j, :, :128]
                row_grad = jnp.concatenate([row_grad[:, : size - 128], edge], axis=1)
            made[0, :, :, start : start + size] = row_grad.astype(jnp.bfloat16).reshape(
                16, SLOTS, size
            )

    def outputs(j):
        for start, size in COLUMNS:
            value = jnp.dot(
                hidden[j], down[j, :, start : start + size], preferred_element_type=jnp.float32
            )
            made[1, :, :, start : start + size] = value.astype(jnp.bfloat16).reshape(
                16, SLOTS, size
            )

    keep_rows(0).start()
    inner_products(0)
    advance(second, 2)
    relay[0].pass_on()
    activations(0)
    outputs(0)
    keep(0)[1].start()
    keep(0)[2].start()
    advance(second, 2)
    dispatch[1].rest()
    relay[1].pass_on()
    keep_rows(1).start()
    inner_products(1)
    activations(1)
    relay[0].from_sides()
    keep(0)[1].wait()
    outputs(1)
    keep(1)[1].start()
    keep(1)[2].start()
    raw_grads(0)
    activation_grads(0)
    row_grads(0, COLUMNS)
    keep(0)[0].start()
    keep(0)[3].start()
    relay[1].from_sides()
    raw_grads(1)
    activation_grads(1)
    keep(0)[0].wait()
    row_grads(1, COLUMNS)
    keep(1)[0].start()
    keep(1)[3].start()
    for copy in keep(0)[2:] + keep(1):
        copy.wait()
    keep_rows(0).wait()
    keep_rows(1).wait()
    for one in dispatch + relay:
        one.sent()


def experts_forward_back(own_rank, own_gates, rows, grads, gate_weight, up_weight, down_weight,
                         gate_bias, up_bias, down_bias, collective_id):
    table = (2, 16, SLOTS, WIDTH)
    all_rows = 2 * HALF_ROWS
    return pl.pallas_call(
        experts_kernel,
        out_shape=(
            jax.ShapeDtypeStruct((2,) + table, jnp.bfloat16),
            jax.ShapeDtypeStruct(table, jnp.bfloat16),
            jax.ShapeDtypeStruct((2, all_rows, LANES), jnp.bfloat16),
            jax.ShapeDtypeStruct((2, all_rows, 2 * LANES), jnp.bfloat16),
            jax.ShapeDtypeStruct(table, jnp.bfloat16),
        ),
        in_specs=[INSIDE] * 3 + [ANYWHERE] * 4 + [INSIDE] * 3,
        out_specs=(ANYWHERE,) * 5,
        scratch_shapes=[
            VMEM((2, 1, 2 * LANES), jnp.float32),
            VMEM((4, 2, SLOTS, WIDTH), jnp.bfloat16),
            VMEM((8 * SLOTS, own_rank.shape[1]), jnp.bfloat16),
            VMEM(table, jnp.bfloat16),
            VMEM((3, HIDDEN, MODEL), jnp.bfloat16),
            VMEM((2, 2 * LANES, WIDTH), jnp.bfloat16),
            VMEM((2, LANES, WIDTH), jnp.bfloat16),
            VMEM((2, 8, SLOTS, WIDTH), jnp.bfloat16),
            VMEM((2, all_rows, LANES), jnp.float32),
            VMEM((2, all_rows, 2 * LANES), jnp.float32),
            VMEM((2, all_rows, LANES), jnp.bfloat16),
            VMEM((2, all_rows, LANES), jnp.bfloat16),
            VMEM((2, all_rows, 2 * LANES), jnp.bfloat16),
            VMEM((2, 16, SLOTS, WIDTH), jnp.bfloat16),
        ]
        + DISPATCH_SEMS
        + DISPATCH_SEMS
        + [DMA((3,)), DMA((2,)), DMA((2,)), DMA((6,))],
        compiler_params=pltpu.CompilerParams(
            collective_id=collective_id, has_side_effects=True, vmem_limit_bytes=60 * MIB
        ),
        name="experts_forward_back",
    )(
        own_rank, own_gates, rows, grads, gate_weight, up_weight, down_weight, gate_bias, up_bias,
        down_bias,
    )


class GiveBack:
    def __init__(self, legs, n, j, parts, out, held, swapped, beside_in, load_sem, core, side, yz):
        self.legs, self.parts, self.out = legs, parts.at[n, j], out
        self.n, self.j = n, j
        self.held, self.swapped = held.at[n, j], swapped.at[n, j]
        self.beside_in = beside_in.at[j]
        self.load_sem, self.core, self.side, self.yz = load_sem, core, side, yz

    def load(self, r, i):
        slot = slot_of(around(self.legs.x, r), self.legs.c, i)
        return pltpu.make_async_copy(
            self.parts.at[slot], self.held.at[r, i], self.load_sem.at[self.n, self.j, 2 * r + i]
        )

    def across(self, r, i):
        slot = slot_of(around(self.legs.x, r), 1 - self.legs.c, i)
        at = (self.n, self.j, 2 * r + i)
        return remote(
            self.parts.at[slot], self.swapped.at[r, i],
            self.core.at[(0,) + at], self.core.at[(1,) + at], self.legs.sibling,
        )

    def aside(self, direction, i):
        at = (self.n, self.j, 2 * direction + i)
        return remote(
            self.held.at[3 if direction == 0 else 1, i], self.beside_in.at[direction, i],
            self.side.at[(0,) + at], self.side.at[(1,) + at], self.legs.beside[direction],
        )

    def leg(self, k):
        a, i = divmod(k, 2)
        at = (self.n, self.j, k)
        return remote(
            self.held.at[2 * a, i], self.out_rows(k),
            self.yz.at[(0,) + at], self.yz.at[(1,) + at], self.legs.there[k],
        )

    def kept(self, k):
        a, i = divmod(k, 2)
        return pltpu.make_async_copy(
            self.held.at[2 * a, i], self.out_rows(k),
            self.yz.at[1, self.n, self.j, k],
        )

    def out_rows(self, k):
        return self.out.at[pl.ds((2 * k + self.j) * SLOTS, SLOTS)]

    def start_leg(self, k):
        self.legs.either(k, lambda: self.kept(k).start(), lambda: self.leg(k).start())

    def landed(self, k):
        self.legs.either(k, lambda: self.kept(k).wait(), lambda: self.leg(k).wait_recv())

    def fetch(self):
        for r in (3, 1, 2, 0):
            for i in (0, 1):
                self.across(r, i).start()
                self.load(r, i).start()

    def join(self, r, i):
        self.load(r, i).wait()
        self.across(r, i).wait_recv()
        add_into(self.held.at[r, i], (self.held.at[r, i], self.swapped.at[r, i]), SLOTS)

    def outward(self):
        for i in (0, 1):
            for r, direction in ((3, 0), (1, 1)):
                self.join(r, i)
                self.aside(direction, i).start()

    def onward(self):
        for i in (0, 1):
            self.join(2, i)
            self.start_leg(2 + i)
        for i in (0, 1):
            self.join(0, i)

    def finish(self):
        for i in (0, 1):
            self.aside(0, i).wait_recv()
            self.aside(1, i).wait_recv()
            add_into(
                self.held.at[0, i],
                (self.held.at[0, i], self.beside_in.at[0, i], self.beside_in.at[1, i]),
                SLOTS,
            )
            self.start_leg(i)

    def swapped_out(self):
        for i in (0, 1):
            for r in range(4):
                self.across(r, i).wait_send()

    def sent(self, with_core=True):
        if with_core:
            self.swapped_out()
        for i in (0, 1):
            for direction in (0, 1):
                self.aside(direction, i).wait_send()
        for k in range(4):
            self.legs.either(k, lambda: None, lambda k=k: self.leg(k).wait_send())


def joined_tokens(returned, marks, with_gates, put):
    marks_of = marks[...]
    experts = expert_rows((8, 128), 64) + expert_rows((8, 128), 96)
    experts = jnp.concatenate(
        [jnp.broadcast_to(experts[b : b + 1], (SLOTS, 128)) for b in range(8)], axis=0
    )
    for start, size in COLUMNS:
        block = returned[:HALF_ROWS, start : start + size]
        last = with_gates and start + size == WIDTH
        if last:
            edge = block[:, size - 128 :].astype(jnp.float32)
            lane = lax.broadcasted_iota(jnp.int32, edge.shape, 1)
            high = jnp.sum(jnp.where(lane == 64, edge, 0.0), axis=1, keepdims=True)
            low = jnp.sum(jnp.where(lane == 96, edge, 0.0), axis=1, keepdims=True)
            edge = jnp.where(
                lane < 64, edge, experts * jnp.where(lane < 96, high, low)
            ).astype(jnp.bfloat16)
            block = jnp.concatenate([block[:, : size - 128], edge], axis=1)
        value = lax.dot_general(
            marks_of, block, (((0,), (0,)), ((), ())), preferred_element_type=jnp.float32
        )
        if last:
            value = jnp.concatenate(
                [value[:, : size - 128], merged_tail(value[:, size - 128 :])], axis=1
            )
        put(start, size, value.astype(jnp.bfloat16).reshape(8, 32, size))


def back_kernel(
    parts, own_rank, rows, grads, hidden, grad_low, sums, joined, weight_grads, bias_grads,
    held, swapped, beside_in, returned, slots, token_part, row_stage, grad_stage, hidden_stage,
    low_stage, low_across, hidden_across, made, from_core, core_sums, from_chip, sum_sem,
    load_sem, core, side, yz, keep_sem, stage_sem, made_sem,
):
    legs = Legs(-1)
    barrier = pltpu.get_barrier_semaphore()
    count = legs.greet(barrier)
    greet(barrier, (legs.e, 2 * around(legs.x, 2) + legs.c))
    back = [
        GiveBack(
            legs, n, j, parts, returned, held, swapped, beside_in, load_sem, core, side, yz
        )
        for n in (0, 1)
        for j in (0, 1)
    ]

    def keep(j):
        return pltpu.make_async_copy(held.at[1, j], joined.at[j], keep_sem.at[j])

    def keep_joined(j):
        for r in (3, 1, 2, 0):
            for i in (0, 1):
                back[2 + j].join(r, i)
        keep(j).start()

    def stages(j):
        return (
            pltpu.make_async_copy(grad_low.at[j], low_stage, stage_sem.at[0]),
            pltpu.make_async_copy(hidden.at[j], hidden_stage, stage_sem.at[1]),
            pltpu.make_async_copy(rows.at[j], row_stage, stage_sem.at[2]),
            pltpu.make_async_copy(grads.at[j], grad_stage, stage_sem.at[3]),
        )

    def made_copy(j, n):
        start, size = COLUMNS[n]
        return pltpu.make_async_copy(
            made.at[n % 2, :, pl.ds(0, size)],
            weight_grads.at[j, :, pl.ds(start, size)],
            made_sem.at[n % 2],
        )

    def weight_steps():
        for copy in stages(0):
            copy.start()
        yield
        for j in (0, 1):
            for copy in stages(j):
                copy.wait()
            low_across[...] = low_stage[...].T
            hidden_across[...] = hidden_stage[...].T
            bias_grads[j] = jnp.sum(low_stage[...].astype(jnp.float32), axis=0, keepdims=True)
            yield
            for n, (start, size) in enumerate(COLUMNS):
                if n >= 2:
                    made_copy(j, n - 2).wait()
                value = jnp.dot(
                    low_across[...],
                    row_stage[:, :, start : start + size].reshape(2 * HALF_ROWS, size),
                    preferred_element_type=jnp.float32,
                )
                made[n % 2, : 2 * LANES, :size] = value.astype(jnp.bfloat16)
                value = jnp.dot(
                    hidden_across[...],
                    grad_stage[:, :, start : start + size].reshape(2 * HALF_ROWS, size),
                    preferred_element_type=jnp.float32,
                )
                made[n % 2, 2 * LANES :, :size] = value.astype(jnp.bfloat16)
                made_copy(j, n).start()
                yield
            if j == 0:
                for copy in stages(1):
                    copy.start()
            for n in (len(COLUMNS) - 2, len(COLUMNS) - 1):
                made_copy(j, n).wait()

    weights = weight_steps()

    def advance(count):
        for _ in range(count):
            next(weights, None)

    pl.semaphore_wait(barrier, count + 1)
    back[0].fetch()
    advance(1)
    fill_slots(slots, own_rank)
    back[0].outward()
    back[1].fetch()
    back[0].onward()
    back[1].outward()
    advance(3)
    back[2].fetch()
    back[1].onward()
    advance(1)
    back[0].finish()
    back[3].fetch()
    keep_joined(0)
    advance(2)
    back[1].finish()
    keep_joined(1)
    advance(2)
    for k in range(4):
        back[0].landed(k)
        back[1].landed(k)

    def put(start, size, values):
        token_part[:, :, start : start + size] = values

    joined_tokens(returned, slots, True, put)
    summing = tensor_sum_steps(32, token_part, sums, from_core, core_sums, from_chip, sum_sem)
    next(summing)
    next(summing)
    advance(3)
    next(summing)
    advance(3)
    next(summing)
    next(summing, None)
    in_turns(weights)
    keep(0).wait()
    keep(1).wait()
    for j in (0, 1):
        back[j].sent()
        back[2 + j].swapped_out()


def experts_back(parts, own_rank, rows, grads, hidden, grad_low, collective_id):
    row_block = (SLOTS, WIDTH)
    all_rows = 2 * HALF_ROWS
    bf16 = jnp.bfloat16
    return pl.pallas_call(
        back_kernel,
        out_shape=(
            jax.ShapeDtypeStruct((8, 32, WIDTH), bf16),
            jax.ShapeDtypeStruct((2, 4, 2) + row_block, bf16),
            jax.ShapeDtypeStruct((2, 3 * LANES, WIDTH), bf16),
            jax.ShapeDtypeStruct((2, 1, 2 * LANES), jnp.float32),
        ),
        in_specs=[ANYWHERE, INSIDE] + [ANYWHERE] * 4,
        out_specs=(INSIDE, ANYWHERE, ANYWHERE, INSIDE),
        scratch_shapes=[
            VMEM((2, 2, 4, 2) + row_block, bf16),
            VMEM((2, 2, 4, 2) + row_block, bf16),
            VMEM((2, 2, 2) + row_block, bf16),
            VMEM((HALF_ROWS, WIDTH), bf16),
            VMEM((8 * SLOTS, own_rank.shape[1]), bf16),
            VMEM((8, 32, WIDTH), bf16),
            VMEM((16,) + row_block, bf16),
            VMEM((16,) + row_block, bf16),
            VMEM((all_rows, LANES), bf16),
            VMEM((all_rows, 2 * LANES), bf16),
            VMEM((2 * LANES, all_rows), bf16),
            VMEM((LANES, all_rows), bf16),
            VMEM((2, 3 * LANES, 512), bf16),
        ]
        + tensor_sum_scratch(32)
        + [
            DMA((2, 2, 8)), DMA((2, 2, 2, 8)), DMA((2, 1, 2, 4)), DMA((2, 1, 2, 4)), DMA((2,)),
            DMA((4,)), DMA((2,)),
        ],
        compiler_params=pltpu.CompilerParams(
            collective_id=collective_id, has_side_effects=True, vmem_limit_bytes=60 * MIB
        ),
        name="experts_back",
    )(parts, own_rank, rows, grads, hidden, grad_low)


def last_kernel(
    weight_grads, bias_grads, output, input_grad, qkv_sums, o_sums, common, rest,
    gate_out, up_out, down_out, down_bias_out, gate_bias_out, up_bias_out,
    output_out, input_out, q_out, k_out, v_out, o_out, router_out, norms_out, rest_out,
):
    j = pl.program_id(0)

    @pl.when((j == 0) & (pl.program_id(1) == 0))
    def _():
        for start in range(0, MODEL, 128):
            size = min(128, MODEL - start)
            output_out[start : start + size, :] = output[:, start : start + size].T
            input_out[start : start + size, :] = input_grad[:, start : start + size].T
        q_out[...] = qkv_sums[:180, :512]
        o_out[...] = o_sums[:180, :]
        kv = qkv_sums[:, 512:].T
        k_out[...] = kv[:HEAD_DIMENSION, :180]
        v_out[...] = kv[HEAD_DIMENSION:, :180]
        router_out[...] = common[:32, :MODEL].astype(jnp.float32)
        tail = common[32:, :MODEL].astype(jnp.float32)
        norms_out[:8, :] = tail[:8]
        for r in range(8):
            size = min(LANES, MODEL - r * LANES)
            norms_out[8:9, r * LANES : r * LANES + size] = rest[r : r + 1, :size]
        rest_out[...] = rest[8:, :]

        gate_bias_out[...] = bias_grads[:, :, :HIDDEN]
        up_bias_out[...] = bias_grads[:, :, LANES : LANES + HIDDEN]

    gate_out[0] = weight_grads[0, :HIDDEN].astype(jnp.float32)
    up_out[0] = weight_grads[0, LANES : LANES + HIDDEN].astype(jnp.float32)
    down = weight_grads[0, 2 * LANES :].astype(jnp.float32)
    down_out[0] = down[:HIDDEN]
    down_bias_out[0] = down[HIDDEN : HIDDEN + 1] + down[HIDDEN + 1 : HIDDEN + 2]


def last_results(weight_grads, bias_grads, *finished):
    columns = 512
    steps = -(-MODEL // columns)
    tokens = finished[0].shape[0]
    wide = pl.BlockSpec((1, 3 * LANES, columns), lambda j, n: (j, 0, n))
    made = pl.BlockSpec((1, HIDDEN, columns), lambda j, n: (j, 0, n))
    f32 = jnp.float32
    shape = jax.ShapeDtypeStruct
    weight = shape((2, HIDDEN, MODEL), f32)
    bias = shape((2, 1, HIDDEN), f32)

    def whole(array):
        return pl.BlockSpec(array.shape, lambda j, n: (0,) * len(array.shape))

    others = (
        bias,
        bias,
        shape((MODEL, tokens), jnp.bfloat16),
        shape((MODEL, tokens), f32),
        shape((180, 512), f32),
        shape((HEAD_DIMENSION, 180), f32),
        shape((HEAD_DIMENSION, 180), f32),
        shape((180, 512), f32),
        shape((32, MODEL), f32),
        shape((16, MODEL), f32),
        shape((8, LANES), f32),
    )
    return pl.pallas_call(
        last_kernel,
        grid=(2, steps),
        out_shape=(weight, weight, weight, shape((2, 1, MODEL), f32)) + others,
        in_specs=[wide] + [whole(array) for array in (bias_grads,) + finished],
        out_specs=(
            made,
            made,
            made,
            pl.BlockSpec((1, 1, columns), lambda j, n: (j, 0, n)),
        )
        + tuple(whole(array) for array in others),
        compiler_params=pltpu.CompilerParams(
            dimension_semantics=("arbitrary", "arbitrary"), vmem_limit_bytes=60 * MIB
        ),
        name="last_results",
    )(weight_grads, bias_grads, *finished)


def plain_add(dst, sources, rows):
    def step(i, carry):
        at = pl.ds(pl.multiple_of(i * 16, 16), 16)
        total = sources[0][at, :].astype(jnp.float32)
        for source in sources[1:]:
            total = total + source[at, :].astype(jnp.float32)
        dst[at, :] = total.astype(dst.dtype)
        return carry

    lax.fori_loop(0, rows // 16, step, 0)


def scatter_steps(part, out, half_in, full_in, totals, send, recv):
    z, y, x, c = place()
    t = 2 * x + c
    half = SHARD_ROWS // 2
    quarter = half // 2

    def at(axis, by, other):
        if axis == 0:
            return around(z, by) * SIDE + around(y, other)
        return around(z, other) * SIDE + around(y, by)

    def ring(h, n, axis, chunk):
        def early(k):
            by = (1, -1)[k]
            return remote(
                chunk(2).at[pl.ds(k * quarter, quarter)], half_in.at[h, n, k],
                send.at[h, n, k], recv.at[h, n, k], (at(axis, by, 0), t),
            )

        def late(k):
            by = (1, -1)[k]
            return remote(
                chunk(by), full_in.at[h, n, k],
                send.at[h, n, 2 + k], recv.at[h, n, 2 + k], (at(axis, by, 0), t),
            )

        def add_early(k):
            mine = chunk((1, -1)[k]).at[pl.ds(k * quarter, quarter)]
            plain_add(mine, (mine, half_in.at[h, n, k]), quarter)

        def add_late(dst):
            plain_add(dst, (chunk(0), full_in.at[h, n, 0], full_in.at[h, n, 1]), half)

        return early, late, add_early, add_late

    def wide(h, item):
        return ring(
            h, item % 4, h, lambda by: part.at[at(h, by, item), pl.ds(h * half, half)]
        )

    def narrow(h):
        return ring(h, 4, 1 - h, lambda by: totals.at[h, by % 4])

    items = (2, 1, -1, 0)
    first = [{item: wide(h, item) for item in items} for h in (0, 1)]
    second = [narrow(h) for h in (0, 1)]
    for item in items:
        for h in (0, 1):
            for k in (0, 1):
                first[h][item][0](k).start()
    yield
    for item in items:
        for k in (0, 1):
            for h in (0, 1):
                first[h][item][0](k).wait_recv()
                first[h][item][2](k)
                first[h][item][1](k).start()
        yield
    for item in items:
        for h in (0, 1):
            for k in (0, 1):
                first[h][item][1](k).wait_recv()
            first[h][item][3](totals.at[h, item % 4])
            if item == 2:
                for k in (0, 1):
                    second[h][0](k).start()
        yield
    for k in (0, 1):
        for h in (0, 1):
            second[h][0](k).wait_recv()
            second[h][2](k)
            second[h][1](k).start()
    yield
    for h in (0, 1):
        for k in (0, 1):
            second[h][1](k).wait_recv()
        second[h][3](out.at[pl.ds(h * half, half)])
    yield
    for h in (0, 1):
        for steps in [first[h][item] for item in items] + [second[h]]:
            for k in (0, 1):
                steps[0](k).wait_send()
                steps[1](k).wait_send()


def scatter_scratch(columns):
    half = SHARD_ROWS // 2
    return [
        VMEM((2, 5, 2, half // 2, columns), jnp.bfloat16),
        VMEM((2, 5, 2, half, columns), jnp.bfloat16),
        VMEM((2, 4, half, columns), jnp.bfloat16),
        DMA((2, 5, 4)),
        DMA((2, 5, 4)),
    ]


COMMON_ROWS = 48
REST_ROWS = 16


def small_steps(common, rest, common_out, rest_out, mine, got, kept, others, send, t_send):
    z, y, x, c = place()
    e = z * SIDE + y
    t = 2 * x + c
    own_lanes = pl.ds(pl.multiple_of(t * LANES, 128), LANES)

    def share(d):
        return remote(
            mine, got.at[e], send.at[0, d], send.at[1, d], (lax.rem(e + d, 16), t)
        )

    def shared(d):
        there = got.at[lax.rem(e - d + 16, 16)]
        return remote(there, there, send.at[0, d], send.at[1, d], (lax.rem(e + d, 16), t))

    def spread(d):
        return remote(
            kept, common_out.at[:, own_lanes], t_send.at[0, d], t_send.at[1, d],
            (e, lax.rem(t + d, 8)),
        )

    def spread_in(d):
        lanes = pl.ds(pl.multiple_of(lax.rem(t - d + 8, 8) * LANES, 128), LANES)
        there = common_out.at[:, lanes]
        return remote(there, there, t_send.at[0, d], t_send.at[1, d], (e, lax.rem(t + d, 8)))

    def part(d):
        return remote(
            others.at[t], others.at[t], t_send.at[2, d], t_send.at[3, d],
            (e, lax.rem(t + d, 8)),
        )

    def part_in(d):
        there = others.at[lax.rem(t - d + 8, 8)]
        return remote(there, there, t_send.at[2, d], t_send.at[3, d], (e, lax.rem(t + d, 8)))

    mine[:COMMON_ROWS] = common[:, own_lanes]
    mine[COMMON_ROWS:] = rest[...]
    for d in range(1, 16):
        share(d).start()
    got[e] = mine[...]
    yield
    for d in range(1, 16):
        shared(d).wait_recv()
    total = got[0].astype(jnp.float32)
    for i in range(1, 16):
        total = total + got[i].astype(jnp.float32)
    own = total[:COMMON_ROWS].astype(jnp.bfloat16)
    kept[...] = own
    others[t] = total[COMMON_ROWS:].astype(jnp.bfloat16)
    for d in range(1, 8):
        spread(d).start()
        part(d).start()
    common_out[:, own_lanes] = own
    rest_out[...] = total[COMMON_ROWS:]
    yield
    for d in range(1, 8):
        spread_in(d).wait_recv()
        part_in(d).wait_recv()
    whole = others[0, :8, :].astype(jnp.float32)
    for i in range(1, 8):
        whole = whole + others[i, :8, :].astype(jnp.float32)
    rest_out[:8, :] = whole
    yield
    for d in range(1, 8):
        spread(d).wait_send()
        part(d).wait_send()
    for d in range(1, 16):
        share(d).wait_send()


def lanes_of_shards(m):
    first = 360 * m // 128 * 128
    last = -(-(360 * m + 360) // 128) * 128
    return first, min(last, WIDTH) - first


def into_shards(natural, shards):
    for m in range(8):
        first, size = lanes_of_shards(m)
        source = lax.broadcasted_iota(jnp.int32, (size, LANES), 0) + first
        lane = lax.broadcasted_iota(jnp.int32, (size, LANES), 1)
        inner = jnp.where(lane >= SHARD_ROWS, lane - SHARD_ROWS, lane)
        wanted = 360 * m + inner + jnp.where(lane >= SHARD_ROWS, 180, 0)
        ones = jnp.where((inner < 180) & (source == wanted), 1.0, 0.0).astype(jnp.bfloat16)
        moved = jnp.dot(
            natural[:, first : first + size], ones, preferred_element_type=jnp.float32
        )
        shards[:, m * LANES : (m + 1) * LANES] = moved.astype(jnp.bfloat16)


def from_shards(shards, rows, put):
    for start in range(0, WIDTH, LANES):
        size = min(LANES, WIDTH - start)
        valid = min(start + size, MODEL)
        low = start // 180 * SHARD_ROWS + start % 180
        high = (valid - 1) // 180 * SHARD_ROWS + (valid - 1) % 180 + 1
        first = low // 128 * 128
        window = -(-high // 128) * 128 - first
        source = lax.broadcasted_iota(jnp.int32, (window, size), 0) + first
        lane = lax.broadcasted_iota(jnp.int32, (window, size), 1) + start
        wanted = lane
        for n in range(start // 180 + 1, (valid - 1) // 180 + 1):
            wanted = jnp.where(lane >= 180 * n, lane + 12 * n, wanted)
        if start // 180:
            wanted = jnp.where(lane < 180 * (start // 180 + 1), lane + 12 * (start // 180), wanted)
        ones = jnp.where((lane < MODEL) & (source == wanted), 1.0, 0.0).astype(jnp.bfloat16)
        moved = jnp.dot(
            shards[:rows, first : first + window], ones,
            preferred_element_type=jnp.float32,
        )
        put(start, size, moved.astype(jnp.bfloat16))


def rotated(values, cosines, sines):
    lane = lax.broadcasted_iota(jnp.int32, values.shape, 1)
    first_half = lax.rem(lane, HEAD_DIMENSION) < HEAD_DIMENSION // 2
    other = jnp.where(first_half, pltpu.roll(values, 96, 1), pltpu.roll(values, 32, 1))
    return values * cosines + other * sines


def normal_rows(values):
    mean = jnp.sum(values * values, axis=1, keepdims=True) * (1.0 / MODEL)
    scale = lax.rsqrt(mean + EPSILON)
    return scale, values * scale


def over_rows(body, rows):
    lax.fori_loop(
        0, rows // 16, lambda i, carry: body(i, pl.ds(pl.multiple_of(i * 16, 16), 16)) or carry, 0
    )


def lane_value(values, lane_index):
    lane = lax.broadcasted_iota(jnp.int32, values.shape, 1)
    return jnp.sum(jnp.where(lane == lane_index, values, 0.0), axis=1, keepdims=True)


def block_rows(ref, i):
    return ref[lax.div(i, 2), pl.ds(pl.multiple_of(lax.rem(i, 2) * 16, 16), 16), :]


def forward_kernel(
    q_across, key_matrix, value_matrix, o_across, routes, cotangent_across, layer_across,
    segments, vectors, cosines, sines, router,
    qkv_weight, out_weight, grads, own_rank, own_gates, gate_table, middle, moe_in, queries, kv,
    log_total, attn_low, allowed, layer_input, cotangent, router_rows,
    qkv_shard, o_shard, blocks, slots, natural, shards, halo, out_part, out_sum, halo_sem,
    yz, own_sem, send, recv, *scratch
):
    legs = Legs(1)
    e, t = legs.e, legs.t
    tokens = layer_input.shape[0]
    shard_width = q_across.shape[0]
    qkv_shard[...] = jnp.zeros_like(qkv_shard)
    o_shard[...] = jnp.zeros_like(o_shard)
    qkv_shard[:shard_width, :512] = q_across[...]
    o_shard[:shard_width, :] = o_across[...]
    key_value = jnp.concatenate(
        [key_matrix[...].astype(jnp.float32), value_matrix[...].astype(jnp.float32)], axis=0
    )
    qkv_shard[:shard_width, 512:] = key_value.T.astype(jnp.bfloat16)
    window = WINDOW_LENGTH
    score_scale = HEAD_DIMENSION ** (-0.5)
    qkv_gather = Gather(qkv_shard, qkv_weight, own_sem.at[0], send.at[0], recv.at[0])
    o_gather = Gather(o_shard, out_weight, own_sem.at[1], send.at[1], recv.at[1])
    barrier = pltpu.get_barrier_semaphore()
    count = legs.greet(barrier)
    for partner in qkv_gather.partners():
        greet(barrier, partner)
    greet(barrier, (e, 2 * around(legs.x, 2) + legs.c))
    greet(barrier, (lax.rem(e + 1, 16), t))
    greet(barrier, (lax.rem(e + 15, 16), t))
    pl.semaphore_wait(barrier, count + 7)
    qkv_steps, o_steps = qkv_gather.steps(), o_gather.steps()
    out_steps = tensor_sum_steps(32, out_part, out_sum, *scratch)

    def leg(k):
        return remote(blocks.at[k], grads.at[k], yz.at[0, k], yz.at[1, k], legs.there[k])

    def kept(k):
        return pltpu.make_async_copy(blocks.at[k], grads.at[k], yz.at[1, k])

    next(qkv_steps)
    next(qkv_steps)

    for start in range(0, MODEL, 128):
        size = min(128, MODEL - start)
        layer_input[:, start : start + size] = layer_across[start : start + size, :].T
    next(qkv_steps)
    next(o_steps)
    natural[:, EDGE:] = jnp.zeros((tokens, 128), jnp.bfloat16)

    def normed_rows(i, at):
        _, normal_one = normal_rows(layer_input[at, :].astype(jnp.float32))
        natural[at, :MODEL] = (normal_one * vectors[0:1, :MODEL]).astype(jnp.bfloat16)

    over_rows(normed_rows, tokens)
    next(qkv_steps)
    into_shards(natural, shards)
    next(qkv_steps)
    next(o_steps)
    next(qkv_steps)
    lane = lax.broadcasted_iota(jnp.int32, (tokens, 128), 1)
    expert = lax.broadcasted_iota(jnp.int32, (128, tokens), 0)
    marks_across = jnp.zeros((128, tokens), jnp.float32)
    for k in range(TOP):
        marks_across = jnp.where(routes[k : k + 1, :] == expert, 1.0, marks_across)
    marks = marks_across.T
    row = lax.broadcasted_iota(jnp.int32, (tokens, tokens), 0)
    column = lax.broadcasted_iota(jnp.int32, (tokens, tokens), 1)
    before = (row < column).astype(jnp.float32).astype(jnp.bfloat16)
    rank = jnp.dot(
        marks_across.astype(jnp.bfloat16), before, preferred_element_type=jnp.float32
    )
    rank = jnp.where(marks_across > 0.0, rank, -1.0).astype(jnp.bfloat16)
    own_rank[...] = jnp.dot(
        expert_rows((8, 128), 0).astype(jnp.bfloat16), rank, preferred_element_type=jnp.float32
    )
    fill_slots(slots, own_rank)
    router_rows[...] = jnp.zeros_like(router_rows)
    router_rows[: router.shape[0], :MODEL] = router[...]

    def segment_row(by):
        index = jnp.maximum(2 * e + by, 0)
        return segments[pl.ds(index, 1), :].astype(jnp.float32)

    key_segments = jnp.concatenate([segment_row(by) for by in (-1, 0, 1)], axis=1)
    own_segments = jnp.concatenate(
        [jnp.broadcast_to(segment_row(by), (128, 128)).T for by in (0, 1)], axis=0
    )
    place_of = lax.broadcasted_iota(jnp.int32, (tokens, tokens + window), 0)
    key_place = lax.broadcasted_iota(jnp.int32, (tokens, tokens + window), 1) - window
    live = (
        (place_of >= key_place)
        & (place_of - key_place < window)
        & (key_place + e * tokens >= 0)
        & (own_segments[:, :1] == key_segments)
    )
    allowed[...] = live.astype(jnp.float32)
    next(qkv_steps, None)
    next(o_steps)
    qkv = (
        jnp.dot(
            shards[...], qkv_weight[...].reshape(16 * SHARD_ROWS, 640),
            preferred_element_type=jnp.float32,
        )
        + vectors[3:4, :640]
    )
    own = qkv[:, 512:]
    own_lane = lax.broadcasted_iota(jnp.int32, own.shape, 1)
    own = jnp.where(
        own_lane < HEAD_DIMENSION, rotated(own, cosines[...], sines[...]), own
    ).astype(jnp.bfloat16)
    kv[window:, :] = own
    halo[...] = own[tokens - window :]
    halo_copy = remote(
        halo, kv.at[pl.ds(0, window)], halo_sem.at[0], halo_sem.at[1], (lax.rem(e + 1, 16), t)
    )
    halo_copy.start()
    for pair in range(4):
        tile = slice(pair * 128, pair * 128 + 128)
        queries[:, tile] = rotated(qkv[:, tile], cosines[...], sines[...]).astype(jnp.bfloat16)
    next(o_steps)
    for start in range(0, MODEL, 128):
        size = min(128, MODEL - start)
        cotangent[:, start : start + size] = cotangent_across[start : start + size, :].T
    marks_of = slots[...]
    for start, size in COLUMNS:
        size = min(size, MODEL - start)
        made = jnp.dot(
            marks_of, cotangent[:, start : start + size], preferred_element_type=jnp.float32
        )
        blocks[:, :, :, start : start + size] = made.astype(jnp.bfloat16).reshape(
            4, 2, SLOTS, size
        )
    blocks[:, :, :, MODEL:] = jnp.zeros((4, 2, SLOTS, WIDTH - MODEL), jnp.bfloat16)
    halo_copy.wait_recv()
    logs = jnp.zeros((tokens, 128), jnp.float32)
    keys, values = kv[:, :HEAD_DIMENSION], kv[:, HEAD_DIMENSION:]
    for pair in range(4):
        tile = slice(pair * 128, pair * 128 + 128)
        made = []
        for part in range(2):
            head = 2 * pair + part
            query = queries[:, tile][:, part * HEAD_DIMENSION : (part + 1) * HEAD_DIMENSION]
            scores = (
                lax.dot_general(
                    query, keys, (((1,), (1,)), ((), ())), preferred_element_type=jnp.float32
                )
                * score_scale
            )
            scores = jnp.where(allowed[...] > 0.0, scores, NEGATIVE)
            sink = lane_value(vectors[4:5, :128], head)
            row_top = jnp.maximum(jnp.max(scores, axis=1, keepdims=True), sink)
            weights = jnp.exp(scores - row_top)
            total = jnp.sum(weights, axis=1, keepdims=True) + jnp.exp(sink - row_top)
            logs = jnp.where(lane == head, row_top + jnp.log(total), logs)
            probs = (weights / total).astype(jnp.bfloat16)
            made.append(jnp.dot(probs, values, preferred_element_type=jnp.float32))
        attn_low[:, tile] = jnp.concatenate(made, axis=1).astype(jnp.bfloat16)
        next(o_steps, None)
        if pair == 2:
            for k in range(4):
                legs.either(k, lambda k=k: kept(k).start(), lambda k=k: leg(k).start())
    log_total[...] = logs
    next(o_steps, None)
    for m in range(8):
        value = lax.dot_general(
            attn_low[...], out_weight[2 * m : 2 * m + 2].reshape(LANES, 512),
            (((1,), (1,)), ((), ())), preferred_element_type=jnp.float32,
        )
        shards[:, m * LANES : (m + 1) * LANES] = value.astype(jnp.bfloat16)

    def put(start, size, moved):
        out_part[:, :, start : start + size] = moved.reshape(8, 32, size)

    from_shards(shards, tokens, put)
    in_turns(out_steps)
    moe_in[:, EDGE:] = jnp.zeros((tokens, 128), jnp.bfloat16)

    def middle_rows(i, at):
        attn_out = block_rows(out_sum, i)[:, :MODEL].astype(jnp.float32)
        value = layer_input[at, :].astype(jnp.float32) + attn_out + vectors[2:3, :MODEL]
        middle[at, :] = value
        _, normal_two = normal_rows(value)
        moe_in[at, :MODEL] = (normal_two * vectors[1:2, :MODEL]).astype(jnp.bfloat16)

    over_rows(middle_rows, tokens)
    logits = (
        lax.dot_general(
            moe_in[...], router_rows[...], (((1,), (1,)), ((), ())),
            preferred_element_type=jnp.float32,
        )
        + vectors[5:6, :128]
    )
    top = jnp.max(jnp.where(marks > 0.0, logits, NEGATIVE), axis=1, keepdims=True)
    powers = jnp.where(marks > 0.0, jnp.exp(logits - top), 0.0)
    table = powers / jnp.sum(powers, axis=1, keepdims=True)
    gate_table[...] = table
    experts = expert_rows((8, 128), 0).astype(jnp.bfloat16)
    gates = jnp.zeros((8, tokens), jnp.float32)
    for _ in range(3):
        piece = table.astype(jnp.bfloat16)
        table = table - piece.astype(jnp.float32)
        gates = gates + lax.dot_general(
            experts, piece, (((1,), (1,)), ((), ())), preferred_element_type=jnp.float32
        )
    own_gates[...] = gates
    for k in range(4):
        legs.either(k, lambda k=k: kept(k).wait(), lambda k=k: leg(k).wait())
    halo_copy.wait_send()


def forward(collective_id, *arrays):
    tokens = arrays[5].shape[1]
    bf16, f32 = jnp.bfloat16, jnp.float32
    shape = jax.ShapeDtypeStruct
    eighths = (8, 32, WIDTH)
    return pl.pallas_call(
        forward_kernel,
        out_shape=(
            shape((16, SHARD_ROWS, 640), bf16),
            shape((16, SHARD_ROWS, 512), bf16),
            shape((4, 2, SLOTS, WIDTH), bf16),
            shape((8, tokens), f32),
            shape((8, tokens), f32),
            shape((tokens, 128), f32),
            shape((tokens, MODEL), f32),
            shape((tokens, WIDTH), bf16),
            shape((tokens, 512), bf16),
            shape((tokens + WINDOW_LENGTH, 128), bf16),
            shape((tokens, 128), f32),
            shape((tokens, 512), bf16),
            shape((tokens, tokens + WINDOW_LENGTH), f32),
            shape((tokens, MODEL), bf16),
            shape((tokens, MODEL), bf16),
            shape((128, WIDTH), bf16),
        ),
        in_specs=[INSIDE] * len(arrays),
        out_specs=(INSIDE, INSIDE, ANYWHERE) + (INSIDE,) * 13,
        scratch_shapes=[
            VMEM((SHARD_ROWS, 640), bf16),
            VMEM((SHARD_ROWS, 512), bf16),
            VMEM((4, 2, SLOTS, WIDTH), bf16),
            VMEM((8 * SLOTS, tokens), bf16),
            VMEM((tokens, WIDTH), bf16),
            VMEM((tokens, 16 * SHARD_ROWS), bf16),
            VMEM((WINDOW_LENGTH, 128), bf16),
            VMEM(eighths, bf16),
            VMEM(eighths, bf16),
            DMA((2,)),
        ]
        + [DMA((2, 4)), DMA((2,)), DMA((2, 2, 5, 4)), DMA((2, 2, 5, 4))]
        + tensor_sum_scratch(32),
        compiler_params=pltpu.CompilerParams(
            collective_id=collective_id, has_side_effects=True, vmem_limit_bytes=60 * MIB
        ),
        name="forward",
    )(*arrays)


def backward_kernel(
    grads_back, joined, own_rank, own_gates, cotangent, middle, layer_input, moe_in, gate_table, router_rows,
    vectors, qkv_weight, out_weight, queries, kv, log_total, attn_low, allowed,
    cosines, sines,
    output, input_grad, qkv_out, o_out, common_out, rest_out, returned,
    slots, own_blocks, beside_in, weight, made_part, joined_sem, side, yz, back_sem, weight_sem,
    logit_pieces, column_sums, natural, shards, head_grads, kv_grads, halo, halo_in, qkv_grad,
    common, rest, normed_part, normed_out, made_out, qkv_part, o_part, halo_sem,
    *scratch
):
    z, y, x, c = place()
    e = z * SIDE + y
    t = 2 * x + c
    rows_count = middle.shape[0]
    window = WINDOW_LENGTH
    score_scale = HEAD_DIMENSION ** (-0.5)
    barrier = pltpu.get_barrier_semaphore()
    for d in range(1, 16):
        greet(barrier, (lax.rem(e + d, 16), t))
    for d in range(1, 8):
        greet(barrier, (e, lax.rem(t + d, 8)))
    pl.semaphore_wait(barrier, 22)
    made_sum = tensor_sum_steps(32, made_part, made_out, *scratch[:4])
    normed_sum = tensor_sum_steps(32, normed_part, normed_out, *scratch[4:8])
    o_scatter = scatter_steps(o_part, o_out, *scratch[8:13])
    qkv_scatter = scatter_steps(qkv_part, qkv_out, *scratch[13:18])
    small = small_steps(common, rest, common_out, rest_out, *scratch[18:])
    legs = Legs(-1)

    def own_load(j):
        return pltpu.make_async_copy(joined.at[j, 0], own_blocks.at[j], joined_sem.at[j])

    def aside(j, direction, i):
        n = 2 * direction + i
        return remote(
            joined.at[j, 3 if direction == 0 else 1, i], beside_in.at[j, direction, i],
            side.at[0, j, n], side.at[1, j, n], legs.beside[direction],
        )

    def leg_ends(j, k):
        a, i = divmod(k, 2)
        return (
            own_blocks.at[j, i] if a == 0 else joined.at[j, 2, i],
            returned.at[pl.ds((2 * k + j) * SLOTS, SLOTS)],
        )

    def leg(j, k):
        src, dst = leg_ends(j, k)
        return remote(src, dst, yz.at[0, j, k], yz.at[1, j, k], legs.there[k])

    def kept(j, k):
        src, dst = leg_ends(j, k)
        return pltpu.make_async_copy(src, dst, yz.at[1, j, k])

    def start_leg(j, k):
        legs.either(k, lambda: kept(j, k).start(), lambda: leg(j, k).start())

    def finish(j):
        own_load(j).wait()
        for i in (0, 1):
            aside(j, 0, i).wait_recv()
            aside(j, 1, i).wait_recv()
            add_into(
                own_blocks.at[j, i],
                (own_blocks.at[j, i], beside_in.at[j, 0, i], beside_in.at[j, 1, i]),
                SLOTS,
            )
            start_leg(j, i)

    back_load = pltpu.make_async_copy(returned, natural.at[pl.ds(0, HALF_ROWS)], back_sem)
    for j in (0, 1):
        for i in (0, 1):
            aside(j, 0, i).start()
            aside(j, 1, i).start()
            start_leg(j, 2 + i)
        own_load(j).start()
    out_load = pltpu.make_async_copy(out_weight, weight.at[:, :, :512], weight_sem.at[0])
    qkv_load = pltpu.make_async_copy(qkv_weight, weight, weight_sem.at[1])
    out_load.start()
    fill_slots(slots, own_rank)
    for b in range(8):
        at = slice(b * SLOTS, (b + 1) * SLOTS)
        gates = slots[at, :].astype(jnp.float32) * own_gates[b : b + 1, :]
        slots[at, :] = gates.astype(jnp.bfloat16)

    column_sums[...] = jnp.zeros_like(column_sums)
    natural[:, EDGE:] = jnp.zeros((2 * rows_count, 128), jnp.bfloat16)

    def logits(i, at):
        tail = block_rows(grads_back, i)[:, EDGE:].astype(jnp.float32)
        lane = lax.broadcasted_iota(jnp.int32, tail.shape, 1)
        gate_grad = jnp.where(lane < 32, pltpu.roll(tail, 64, 1) + pltpu.roll(tail, 32, 1), 0.0)
        table = gate_table[at, :]
        logit_grad = table * (
            gate_grad - jnp.sum(table * gate_grad, axis=1, keepdims=True)
        )
        high = logit_grad.astype(jnp.bfloat16)
        rest_of = logit_grad - high.astype(jnp.float32)
        mid = rest_of.astype(jnp.bfloat16)
        logit_pieces[at, :128] = high
        logit_pieces[at, 128:256] = mid
        logit_pieces[at, 256:] = (rest_of - mid.astype(jnp.float32)).astype(jnp.bfloat16)

    over_rows(logits, rows_count)
    for start, size in COLUMNS:
        size = min(size, MODEL - start)
        router = router_rows[:, start : start + size]
        input_grad[:, start : start + size] = sum(
            jnp.dot(
                logit_pieces[:, n * 128 : n * 128 + 128], router,
                preferred_element_type=jnp.float32,
            )
            for n in range(3)
        )

    def middle_rows(i, at):
        moe_in_grad = block_rows(grads_back, i)[:, :MODEL].astype(jnp.float32) + input_grad[at, :]
        scale_two, normal_two = normal_rows(middle[at, :])
        scaled = moe_in_grad * vectors[1:2, :MODEL]
        mean = jnp.sum(scaled * normal_two, axis=1, keepdims=True) * (1.0 / MODEL)
        middle_grad = cotangent[at, :].astype(jnp.float32) + scale_two * (
            scaled - normal_two * mean
        )
        column_sums[0] = column_sums[0] + middle_grad
        column_sums[1] = column_sums[1] + moe_in_grad * normal_two
        input_grad[at, :] = middle_grad
        natural[at, :MODEL] = middle_grad.astype(jnp.bfloat16)
        _, normal_one = normal_rows(layer_input[at, :].astype(jnp.float32))
        below = pl.ds(pl.multiple_of(rows_count + i * 16, 16), 16)
        natural[below, :MODEL] = (normal_one * vectors[0:1, :MODEL]).astype(jnp.bfloat16)

    over_rows(middle_rows, rows_count)
    into_shards(natural, shards)
    finish(0)

    def part_from(top, right, part):
        for m in range(8):
            value = lax.dot_general(
                shards[top : top + rows_count, m * LANES : (m + 1) * LANES], right,
                (((0,), (0,)), ((), ())), preferred_element_type=jnp.float32,
            )
            part[2 * m : 2 * m + 2] = value.astype(jnp.bfloat16).reshape(
                2, SHARD_ROWS, right.shape[1]
            )

    part_from(0, attn_low[...], o_part)
    next(o_scatter)
    finish(1)
    out_load.wait()
    head_grads[...] = jnp.dot(
        shards[:rows_count, :], weight[:, :, :512].reshape(16 * SHARD_ROWS, 512),
        preferred_element_type=jnp.float32,
    ).astype(jnp.bfloat16)
    qkv_load.start()
    kv_grads[...] = jnp.zeros_like(kv_grads)
    keys, values = kv[:, :HEAD_DIMENSION], kv[:, HEAD_DIMENSION:]
    sink_lane = lax.broadcasted_iota(jnp.int32, (1, 128), 1)
    sink_grads = jnp.zeros((1, 128), jnp.float32)
    for pair in range(4):
        tile = slice(pair * 128, pair * 128 + 128)
        query_grads = []
        for lower in range(2):
            head = 2 * pair + lower
            part = slice(lower * HEAD_DIMENSION, (lower + 1) * HEAD_DIMENSION)
            query = queries[:, tile][:, part]
            grad = head_grads[:, tile][:, part]
            log_of = lane_value(log_total[...], head)
            scores = (
                lax.dot_general(
                    query, keys, (((1,), (1,)), ((), ())),
                    preferred_element_type=jnp.float32,
                )
                * score_scale
            )
            probs = jnp.where(allowed[...] > 0.0, jnp.exp(scores - log_of), 0.0)
            prob_grad = lax.dot_general(
                grad, values, (((1,), (1,)), ((), ())), preferred_element_type=jnp.float32
            )
            row_dot = jnp.sum(probs * prob_grad, axis=1, keepdims=True)
            score_grad = (probs * (prob_grad - row_dot)).astype(jnp.bfloat16)
            sink = lane_value(vectors[4:5, :128], head)
            sink_grad = -jnp.sum(jnp.exp(sink - log_of) * row_dot, axis=0, keepdims=True)
            sink_grads = jnp.where(sink_lane == head, sink_grad, sink_grads)
            query_grads.append(
                jnp.dot(score_grad, keys, preferred_element_type=jnp.float32) * score_scale
            )
            kv_grads[:, :HEAD_DIMENSION] += (
                lax.dot_general(
                    score_grad, query, (((0,), (0,)), ((), ())),
                    preferred_element_type=jnp.float32,
                )
                * score_scale
            )
            kv_grads[:, HEAD_DIMENSION:] += lax.dot_general(
                probs.astype(jnp.bfloat16), grad, (((0,), (0,)), ((), ())),
                preferred_element_type=jnp.float32,
            )
        qkv_grad[:, tile] = rotated(
            jnp.concatenate(query_grads, axis=1), cosines[...], -sines[...]
        ).astype(jnp.bfloat16)
        next(o_scatter, None)
        if pair == 1:
            for j in (0, 1):
                for k in range(4):
                    legs.either(
                        k, lambda j=j, k=k: kept(j, k).wait(), lambda j=j, k=k: leg(j, k).wait_recv()
                    )
            back_load.start()
        if pair == 2:
            back_load.wait()

            def put_made(start, size, moved):
                made_part[:, :, start : start + size] = moved

            joined_tokens(natural, slots, False, put_made)
            next(made_sum)
        if pair == 3:
            next(made_sum)
        next(o_scatter, None)

    halo[...] = kv_grads[:window, :].astype(jnp.bfloat16)
    halo_copy = remote(
        halo, halo_in, halo_sem.at[0], halo_sem.at[1], (lax.rem(e + 15, 16), t)
    )
    halo_copy.start()

    router_grad = []
    for start, size in COLUMNS:
        size = min(size, MODEL - start)
        value = lax.dot_general(
            logit_pieces[...], moe_in[:, start : start + size], (((0,), (0,)), ((), ())),
            preferred_element_type=jnp.float32,
        )
        value = value[:32] + value[128:160] + value[256:288]
        common[:32, start : start + size] = value.astype(jnp.bfloat16)
        row = lax.broadcasted_iota(jnp.int32, (16, size), 0)
        o_bias = jnp.sum(column_sums[0, :, start : start + size], axis=0, keepdims=True)
        norm = jnp.sum(column_sums[1, :, start : start + size], axis=0, keepdims=True)
        common[32:, start : start + size] = jnp.where(
            row == 0, o_bias, jnp.where(row == 1, norm, 0.0)
        ).astype(jnp.bfloat16)
    row = lax.broadcasted_iota(jnp.int32, (16, 128), 0)
    pieces = logit_pieces[:, :128].astype(jnp.float32)
    pieces = pieces + logit_pieces[:, 128:256].astype(jnp.float32)
    pieces = pieces + logit_pieces[:, 256:].astype(jnp.float32)
    router_bias = jnp.sum(pieces, axis=0, keepdims=True)
    common[32:, :128] = jnp.where(
        row == 2, router_bias, common[32:, :128].astype(jnp.float32)
    ).astype(jnp.bfloat16)
    common[:, MODEL:] = jnp.zeros((COMMON_ROWS, 8 * LANES - MODEL), jnp.bfloat16)

    next(o_scatter, None)
    next(made_sum)
    halo_copy.wait_recv()
    own = kv_grads[window:, :]
    own = jnp.concatenate(
        [own[: rows_count - window], own[rows_count - window :] + halo_in[...].astype(jnp.float32)],
        axis=0,
    )
    lane = lax.broadcasted_iota(jnp.int32, own.shape, 1)
    own = jnp.where(lane < HEAD_DIMENSION, rotated(own, cosines[...], -sines[...]), own)
    qkv_grad[:, 512:] = own.astype(jnp.bfloat16)

    qkv_load.wait()
    for m in range(8):
        value = lax.dot_general(
            qkv_grad[...], weight[2 * m : 2 * m + 2].reshape(LANES, 640),
            (((1,), (1,)), ((), ())), preferred_element_type=jnp.float32,
        )
        shards[:rows_count, m * LANES : (m + 1) * LANES] = value.astype(jnp.bfloat16)

    def put(start, size, moved):
        normed_part[:, :, start : start + size] = moved.reshape(8, 32, size)

    from_shards(shards, rows_count, put)
    next(normed_sum)
    part_from(rows_count, qkv_grad[...], qkv_part)
    next(qkv_scatter)
    next(made_sum)

    column_sums[0] = jnp.zeros((16, MODEL), jnp.float32)

    def norm_rows(i, at):
        _, normal_one = normal_rows(layer_input[at, :].astype(jnp.float32))
        column_sums[0] = column_sums[0] + (
            block_rows(normed_part, i)[:, :MODEL].astype(jnp.float32) * normal_one
        )

    over_rows(norm_rows, rows_count)
    bias_grads = jnp.sum(qkv_grad[...].astype(jnp.float32), axis=0, keepdims=True)
    row = lax.broadcasted_iota(jnp.int32, (REST_ROWS, LANES), 0)
    small_rows = jnp.where(row == 8, bias_grads[:, :LANES], 0.0)
    last = jnp.concatenate([bias_grads[:, LANES:], sink_grads], axis=1)
    small_rows = jnp.where(row == 9, last, small_rows)
    for r in range(8):
        size = min(LANES, MODEL - r * LANES)
        norm = jnp.sum(
            column_sums[0, :, r * LANES : r * LANES + size], axis=0, keepdims=True
        )
        if size < LANES:
            norm = jnp.concatenate([norm, jnp.zeros((1, LANES - size), jnp.float32)], axis=1)
        small_rows = jnp.where(row == r, norm, small_rows)
    rest[...] = small_rows.astype(jnp.bfloat16)
    next(small)
    next(normed_sum)
    for _ in range(4):
        next(qkv_scatter)
    next(normed_sum)
    next(small)
    for _ in range(4):
        next(qkv_scatter)
    next(qkv_scatter)
    next(normed_sum)
    next(small)
    next(qkv_scatter)
    in_turns(normed_sum, qkv_scatter, small, made_sum, o_scatter)
    halo_copy.wait_send()
    for j in (0, 1):
        for i in (0, 1):
            aside(j, 0, i).wait_send()
            aside(j, 1, i).wait_send()
        for k in range(4):
            legs.either(k, lambda: None, lambda j=j, k=k: leg(j, k).wait_send())

    def last_rows(i, at):
        scale_one, normal_one = normal_rows(layer_input[at, :].astype(jnp.float32))
        scaled = block_rows(normed_out, i)[:, :MODEL].astype(jnp.float32) * vectors[0:1, :MODEL]
        mean = jnp.sum(scaled * normal_one, axis=1, keepdims=True) * (1.0 / MODEL)
        input_grad[at, :] = input_grad[at, :] + scale_one * (scaled - normal_one * mean)
        made = block_rows(made_out, i)[:, :MODEL].astype(jnp.float32)
        output[at, :] = (middle[at, :] + made).astype(jnp.bfloat16)

    over_rows(last_rows, rows_count)


def backward(collective_id, *arrays):
    rows_count = arrays[5].shape[0]
    bf16, f32 = jnp.bfloat16, jnp.float32
    tokens = (8, 32, WIDTH)
    return pl.pallas_call(
        backward_kernel,
        out_shape=(
            jax.ShapeDtypeStruct((rows_count, MODEL), bf16),
            jax.ShapeDtypeStruct((rows_count, MODEL), f32),
            jax.ShapeDtypeStruct((SHARD_ROWS, 640), f32),
            jax.ShapeDtypeStruct((SHARD_ROWS, 512), f32),
            jax.ShapeDtypeStruct((COMMON_ROWS, 8 * LANES), bf16),
            jax.ShapeDtypeStruct((REST_ROWS, LANES), f32),
            jax.ShapeDtypeStruct((HALF_ROWS, WIDTH), bf16),
        ),
        in_specs=[
            ANYWHERE if n in (1, 11, 12) else INSIDE for n in range(len(arrays))
        ],
        out_specs=(INSIDE,) * 6 + (ANYWHERE,),
        scratch_shapes=[
            VMEM((8 * SLOTS, rows_count), bf16),
            VMEM((2, 2, SLOTS, WIDTH), bf16),
            VMEM((2, 2, 2, SLOTS, WIDTH), bf16),
            VMEM((16, SHARD_ROWS, 640), bf16),
            VMEM(tokens, bf16),
            DMA((2,)),
            DMA((2, 2, 4)),
            DMA((2, 2, 4)),
            DMA(()),
            DMA((2,)),
            VMEM((rows_count, 3 * 128), bf16),
            VMEM((2, 16, MODEL), f32),
            VMEM((2 * rows_count, WIDTH), bf16),
            VMEM((2 * rows_count, 16 * SHARD_ROWS), bf16),
            VMEM((rows_count, 512), bf16),
            VMEM((rows_count + WINDOW_LENGTH, 128), f32),
            VMEM((WINDOW_LENGTH, 128), bf16),
            VMEM((WINDOW_LENGTH, 128), bf16),
            VMEM((rows_count, 640), bf16),
            VMEM((COMMON_ROWS, 8 * LANES), bf16),
            VMEM((REST_ROWS, LANES), bf16),
            VMEM(tokens, bf16),
            VMEM(tokens, bf16),
            VMEM(tokens, bf16),
            VMEM((16, SHARD_ROWS, 640), bf16),
            VMEM((16, SHARD_ROWS, 512), bf16),
            DMA((2,)),
        ]
        + tensor_sum_scratch(32)
        + tensor_sum_scratch(32)
        + scatter_scratch(512)
        + scatter_scratch(640)
        + [
            VMEM((COMMON_ROWS + REST_ROWS, LANES), bf16),
            VMEM((16, COMMON_ROWS + REST_ROWS, LANES), bf16),
            VMEM((COMMON_ROWS, LANES), bf16),
            VMEM((8, REST_ROWS, LANES), bf16),
            DMA((2, 16)),
            DMA((4, 8)),
        ],
        compiler_params=pltpu.CompilerParams(
            collective_id=collective_id, has_side_effects=True, vmem_limit_bytes=60 * MIB
        ),
        name="backward",
    )(*arrays)


def local(
    layer_input,
    segment_ids,
    expert_routes,
    attn_norm,
    q_weight,
    q_bias,
    key_matrix,
    key_bias,
    value_matrix,
    value_bias,
    o_weight,
    o_bias,
    sink_scores,
    moe_norm,
    router_weight,
    router_bias,
    gate_weight,
    gate_bias,
    up_weight,
    up_bias,
    down_weight,
    down_bias,
    cotangent,
):
    rows_count, model_width = layer_input.shape
    head_size = HEAD_DIMENSION
    window = WINDOW_LENGTH
    q_heads = q_weight.shape[0] // head_size
    q_width, kv_width = q_weight.shape[0], key_matrix.shape[0]
    qkv_width = q_width + 2 * kv_width
    expert_count = router_weight.shape[0]
    sequence_length = rows_count * lax.axis_size("expert")
    expert_index = lax.axis_index("expert")

    places = expert_index * rows_count + jnp.arange(rows_count, dtype=jnp.int32)
    seq_places = places % sequence_length
    frequencies = ROPE_BASE ** (-(2.0 * jnp.arange(head_size // 2, dtype=jnp.float32)) / head_size)
    angles = seq_places.astype(jnp.float32)[:, None] * frequencies[None, :]
    angles = jnp.tile(angles, (1, 4))
    half_signs = jnp.tile(jnp.repeat(jnp.array([-1.0, 1.0], jnp.float32), head_size // 2), 2)
    cosines, sines = jnp.cos(angles), jnp.sin(angles) * half_signs
    wide = 8 * LANES
    vectors = [
        attn_norm, moe_norm, o_bias, jnp.concatenate([q_bias, key_bias, value_bias]), sink_scores,
        router_bias,
    ]
    vectors = jnp.stack([jnp.pad(one, (0, wide - one.shape[0])) for one in vectors])
    (
        qkv_weight, out_weight, grad_blocks, own_rank, own_gates, gate_table, middle, moe_in,
        queries, kv, log_total, attn_low, allowed, layer_rows, cotangent_rows, routers,
    ) = forward(
        1,
        q_weight.T,
        key_matrix,
        value_matrix,
        o_weight.T,
        expert_routes.T,
        cotangent.T,
        layer_input.T,
        segment_ids.reshape(sequence_length // 128, 128),
        vectors,
        cosines,
        sines,
        router_weight,
    )
    parts, arrived_rows, hidden, grad_low, arrived_grad = experts_forward_back(
        own_rank, own_gates, moe_in, grad_blocks, gate_weight.swapaxes(1, 2),
        up_weight.swapaxes(1, 2), down_weight, gate_bias, up_bias, down_bias, 4,
    )
    grads_back, joined, weight_grads, bias_grads = experts_back(
        parts, own_rank, arrived_rows, arrived_grad, hidden, grad_low, 5
    )
    output, input_grad, qkv_shard, o_shard, common, rest, _ = backward(
        6,
        grads_back,
        joined,
        own_rank,
        own_gates,
        cotangent_rows,
        middle,
        layer_rows,
        moe_in,
        gate_table,
        routers,
        vectors,
        qkv_weight,
        out_weight,
        queries,
        kv,
        log_total,
        attn_low,
        allowed,
        cosines,
        sines,
    )
    (
        gate_weight_grad, up_weight_grad, down_weight_grad, down_bias_grad, gate_bias_grad,
        up_bias_grad, output, input_grad, q_grad, k_grad, v_grad, o_grad, router_grad, norms, rest,
    ) = last_results(
        weight_grads, bias_grads, output, input_grad, qkv_shard, o_shard, common, rest
    )
    rest = rest[:2].reshape(-1)
    return (
        output.T,
        input_grad.T,
        norms[8],
        q_grad.T,
        rest[:q_width],
        k_grad,
        rest[q_width : q_width + kv_width],
        v_grad,
        rest[q_width + kv_width : qkv_width],
        o_grad.T,
        norms[0],
        rest[qkv_width : qkv_width + q_heads],
        norms[1],
        router_grad,
        norms[2, :expert_count],
        gate_weight_grad.swapaxes(1, 2),
        gate_bias_grad[:, 0],
        up_weight_grad.swapaxes(1, 2),
        up_bias_grad[:, 0],
        down_weight_grad,
        down_bias_grad[:, 0],
    )


def solution(mesh):
    placed = (
        P("expert", None),
        P(),
        P("expert", None),
        P(),
        P("tensor", "expert"),
        P("tensor"),
        P("tensor", "expert"),
        P("tensor"),
        P("tensor", "expert"),
        P("tensor"),
        P("tensor", "expert"),
        P(),
        P("tensor"),
        P(),
        P(),
        P(),
        P("expert", None, "tensor"),
        P("expert", "tensor"),
        P("expert", None, "tensor"),
        P("expert", "tensor"),
        P("expert", "tensor", None),
        P("expert", None),
        P("expert", None),
    )
    return jax.shard_map(
        local,
        mesh=mesh,
        in_specs=placed,
        out_specs=(
            P("expert", None),
            P("expert", None),
            P(),
            P("tensor", "expert"),
            P("tensor"),
            P("tensor", "expert"),
            P("tensor"),
            P("tensor", "expert"),
            P("tensor"),
            P("tensor", "expert"),
            P(),
            P("tensor"),
            P(),
            P(),
            P(),
            P("expert", None, "tensor"),
            P("expert", "tensor"),
            P("expert", None, "tensor"),
            P("expert", "tensor"),
            P("expert", "tensor", None),
            P("expert", None),
        ),
        check_vma=False,
    )
```
